256 devices in a mesh: dep: 128 (over z, x, y), tp: 2 (over core).
Axes of the slice: x: 4, y: 4, z: 8, core: 2. Of those that a mesh axis runs over, the one named last changes fastest.
Arguments:
- patches: bfloat16 [65536, 1152], P('dep', 'tp'), may hold values from -36 to 36
- image_count: int32 [128], P('dep'), may hold values from 0 to 1, as said below
- text_tokens: bfloat16 [16384, 4096], P('dep', 'tp'), may hold values from -6 to 6
- norm_gain: float32 [1152], replicated, may hold values from 0.1 to 1.9
- norm_bias: float32 [1152], replicated, may hold values from -3 to 3
- patch_proj: bfloat16 [1152, 3, 576], P(None, None, 'tp')
- patch_out: bfloat16 [576, 1152], P('tp'), may hold values from -0.25 to 0.25
- merge_gain: float32 [1152], replicated, may hold values from 0.1 to 1.9
- merge_bias: float32 [1152], replicated, may hold values from -3 to 3
- merger: bfloat16 [4, 1152, 4096], P(None, 'tp', 'dep'), may hold values from -1 to 1
- token_gain: float32 [4096], P('tp'), may hold values from 0.1 to 1.9
- router: bfloat16 [4096, 128], P('tp')
- expert_ids: int32 [16384, 8], P('dep'), may hold values from 0 to 127, as said below
Outputs:
- dispatched: bfloat16 [128, 2048, 4096], P('dep', None, 'tp')
- gate_probs: float32 [16384, 8], P('dep')
The draws below stay inside these ranges and needn't reach their ends.
Inputs may be any that keep to these rules, and one draw needn't show every extreme that they name: `image_count`: in each aligned pair of dep indices (2k, 2k+1) exactly one holds an image. `expert_ids`: among the rows of one index of dep exactly 64 experts are named, each exactly 16 times. One expert is named by the rows of every index of dep, another by the rows of a single index only.
All inputs are finite; a program needn't handle non-finite values.
Results may differ from the reference program's by a relative error of at most 0.013.
Values may be sent and summed in bfloat16 or wider, within the bound.
A program may use at most 192 MiB of HBM per device.

```python
import math
import jax
import jax.numpy as jnp
from jax import lax

V = 1152
VH = 8
VISION_HEAD_SIZE = 72
HEADS_WIDTH = 576
D = 4096
TOPK = 8
EXPERTS = 128
IMAGE_PATCHES = 512
VIS = 128
ROWS = 128
CAP = 16
IMAGES = 128
TOKENS = 16384
N_DEP = 128


def image_pairs(key):
    pair_key, chosen_key = jax.random.split(jax.random.fold_in(key, 7))
    picked = jax.random.randint(pair_key, (IMAGES // 2,), 0, 2).astype(jnp.int32)
    chosen = jax.random.randint(chosen_key, (), 0, IMAGES // 2).astype(jnp.int32)
    holder = (2 * chosen + 1 - picked[chosen]).astype(jnp.int32)
    lonely = ((holder + IMAGES // 2) % EXPERTS).astype(jnp.int32)
    return (picked, holder, lonely)


def draw_image_count(key, part):
    picked, holder, lonely = image_pairs(key)
    return jnp.stack([picked, 1 - picked], axis=1).reshape(IMAGES).astype(jnp.int32)


def draw_patches(key, part):
    key = jax.random.fold_in(key, 15)
    position = jnp.arange(V, dtype=jnp.float32) / (V - 1)
    rise = jnp.exp(position * math.log(6.0))
    values = jnp.clip(jax.random.normal(key, (IMAGES * IMAGE_PATCHES, V), jnp.float32), -6.0, 6.0)
    return (values * rise[None, :]).astype(jnp.bfloat16)


def draw_merger(key, part):
    picked, holder, lonely = image_pairs(key)
    key = jax.random.fold_in(key, 16)
    base_key, scale_key = jax.random.split(key)
    group_scale = jnp.exp(jax.random.uniform(scale_key, (EXPERTS,), jnp.float32, 0.0, math.log(10.0)))
    group_scale = jnp.where(jnp.arange(EXPERTS, dtype=jnp.int32) == lonely, 10.0, group_scale)
    column_scale = jnp.repeat(group_scale, D // EXPERTS, total_repeat_length=D)
    base = jnp.clip(jax.random.normal(base_key, (4, V, D), jnp.float32), -6.0, 6.0)
    weights = base * column_scale[None, None, :] / (4.0 * jnp.sqrt(jnp.float32(4 * V)))
    return weights.astype(jnp.bfloat16)


def draw_patch_proj(key, part):
    key = jax.random.fold_in(key, 12)
    base_key = jax.random.fold_in(key, 0)
    weights = jax.random.normal(base_key, (V, 3, HEADS_WIDTH), jnp.float32) / jnp.sqrt(jnp.float32(V))
    return weights.astype(jnp.bfloat16)


def draw_router(key, part):
    key = jax.random.fold_in(key, 13)
    base_key = jax.random.fold_in(key, 0)
    weights = jax.random.normal(base_key, (D, EXPERTS), jnp.float32) * (3.0 / jnp.sqrt(jnp.float32(D)))
    return weights.astype(jnp.bfloat16)


def draw_expert_ids(key, part):
    picked, holder, lonely = image_pairs(key)
    key = jax.random.fold_in(key, 14)
    shared_key, source_key = jax.random.split(key)
    shared = ((lonely + 1 + jax.random.randint(shared_key, (), 0, EXPERTS - 1)) % EXPERTS).astype(jnp.int32)
    half_count = EXPERTS // 2
    expert_iota = jnp.arange(EXPERTS, dtype=jnp.int32)
    row_iota = jnp.arange(ROWS, dtype=jnp.int32)
    choice_iota = jnp.arange(TOPK, dtype=jnp.int32)

    def one_source(source, source_key):
        order_key, offset_key, row_key = jax.random.split(source_key, 3)
        score = jnp.argsort(jax.random.permutation(order_key, EXPERTS).astype(jnp.int32)).astype(jnp.int32)
        lonely_score = jnp.where(source == holder, -2, EXPERTS + 1).astype(jnp.int32)
        score = jnp.where(expert_iota == lonely, lonely_score, jnp.where(expert_iota == shared, -1, score)).astype(jnp.int32)
        members = jnp.argsort(score)[:half_count].astype(jnp.int32)
        offset = jax.random.randint(offset_key, (), 0, half_count).astype(jnp.int32)
        positions = (offset + row_iota[:, None] * TOPK + choice_iota[None, :]) % half_count
        contains = jnp.any(positions == 0, axis=1)
        ranking = jnp.where(contains, 0, ROWS).astype(jnp.int32) + jax.random.permutation(row_key, ROWS).astype(jnp.int32)
        ordered = positions[jnp.argsort(ranking)]
        return members[ordered]
    source_keys = jax.random.split(source_key, IMAGES)
    ids = jax.vmap(one_source)(jnp.arange(IMAGES, dtype=jnp.int32), source_keys)
    return ids.reshape(TOKENS, TOPK).astype(jnp.int32)


def block_scale(rng, shape, shards, smallest, top_value):
    def one(axis_at, shards_of):
        draws = jax.random.uniform(jax.random.fold_in(jax.random.fold_in(rng, 6), axis_at), (shards_of,), jnp.float32, smallest / len(shards), top_value / len(shards))
        return jnp.repeat(jnp.exp(draws), shape[axis_at] // shards_of).reshape((-1,) + (1,) * (len(shape) - axis_at - 1))

    gain = one(*shards[0])
    for cut in shards[1:]:
        gain = gain * one(*cut)
    return gain


def centred(own_key, dims, width, bound, cuts=(), held_as=jnp.bfloat16):
    drawn = width * jax.random.normal(own_key, dims, jnp.float32)
    if cuts:
        drawn = drawn * block_scale(own_key, dims, cuts, -0.22, 0.18)
    return jnp.clip(drawn, -bound, bound).astype(held_as)


def setup_inputs(seed: int = 0) -> dict:
    arg_keys = jax.random.split(jax.random.key(seed), 14)
    patches = draw_patches(jax.random.fold_in(arg_keys[13], 71), 0)
    image_count = draw_image_count(jax.random.fold_in(arg_keys[13], 71), 0)
    text_tokens = centred(arg_keys[2], (TOKENS, D), 1.0, 6.0, ((0, 128), (1, 2)))
    norm_gain = jnp.clip(1.0 + 0.18 * jax.random.normal(arg_keys[3], (V,), jnp.float32), 0.1, 1.9)
    norm_bias = centred(arg_keys[4], (V,), 0.5, 3.0, (), jnp.float32)
    patch_proj = draw_patch_proj(jax.random.fold_in(arg_keys[13], 71), 0)
    patch_out = centred(arg_keys[6], (HEADS_WIDTH, V), HEADS_WIDTH ** -0.5, 0.25, ((0, 2),))
    merge_gain = jnp.clip(1.0 + 0.18 * jax.random.normal(arg_keys[7], (V,), jnp.float32), 0.1, 1.9)
    merge_bias = centred(arg_keys[8], (V,), 0.5, 3.0, (), jnp.float32)
    merger = draw_merger(jax.random.fold_in(arg_keys[13], 71), 0)
    token_gain = jnp.clip(1.0 + 0.18 * jax.random.normal(arg_keys[10], (D,), jnp.float32), 0.1, 1.9)
    router = draw_router(jax.random.fold_in(arg_keys[13], 71), 0)
    expert_ids = draw_expert_ids(jax.random.fold_in(arg_keys[13], 71), 0)
    return {"patches": patches, "image_count": image_count, "text_tokens": text_tokens, "norm_gain": norm_gain, "norm_bias": norm_bias, "patch_proj": patch_proj, "patch_out": patch_out, "merge_gain": merge_gain, "merge_bias": merge_bias, "merger": merger, "token_gain": token_gain, "router": router, "expert_ids": expert_ids}


EPS = 1e-06

def rounded(values_in):
    return lax.optimization_barrier(values_in.astype(jnp.bfloat16)).astype(jnp.float32)

def layer_stats_norm(values_in, gain_vec, bias_vec):
    feature_count = values_in.shape[-1]
    row_mean = lax.optimization_barrier(jnp.sum(values_in, -1, keepdims=True)) / feature_count
    row_var = lax.optimization_barrier(jnp.sum(values_in * values_in, -1, keepdims=True)) / feature_count - row_mean * row_mean
    return (values_in - row_mean) * lax.rsqrt(row_var + EPS) * gain_vec + bias_vec

def vision_image(image_rows, norm_gain, norm_bias, patch_proj, patch_out, merge_gain, merge_bias, merger):
    pixels_in = image_rows.astype(jnp.float32)
    normed_in = layer_stats_norm(pixels_in, norm_gain, norm_bias).astype(jnp.bfloat16)
    projected = jnp.dot(normed_in, patch_proj.reshape(V, 3 * HEADS_WIDTH), preferred_element_type=jnp.float32).astype(jnp.bfloat16)
    query_rows = projected[:, :HEADS_WIDTH].astype(jnp.float32).reshape(IMAGE_PATCHES, VH, VISION_HEAD_SIZE)
    key_matrix = projected[:, HEADS_WIDTH:2 * HEADS_WIDTH].astype(jnp.float32).reshape(IMAGE_PATCHES, VH, VISION_HEAD_SIZE)
    value_matrix = projected[:, 2 * HEADS_WIDTH:].astype(jnp.float32).reshape(IMAGE_PATCHES, VH, VISION_HEAD_SIZE)
    attention_logits = jnp.einsum('ylj,glj->lyg', query_rows, key_matrix) / math.sqrt(VISION_HEAD_SIZE)
    attention_weights = rounded(jax.nn.softmax(attention_logits, axis=-1))
    attended_output = jnp.einsum('irs,siy->riy', attention_weights, value_matrix).reshape(IMAGE_PATCHES, HEADS_WIDTH).astype(jnp.bfloat16)
    residual = pixels_in + jnp.dot(attended_output, patch_out, preferred_element_type=jnp.float32)
    merged_in = layer_stats_norm(residual, merge_gain, merge_bias).astype(jnp.bfloat16)
    premerge = merged_in.reshape(VIS, 4 * V)
    return jnp.dot(premerge, merger.reshape(4 * V, D), preferred_element_type=jnp.float32).astype(jnp.bfloat16)

def dispatch_rows(operands):
    token_rows, expert_rows = operands
    flat_ids = expert_rows.reshape(-1).astype(jnp.int32)
    onehot = (flat_ids[:, None] == jnp.arange(EXPERTS, dtype=jnp.int32)[None, :]).astype(jnp.int32)
    before = (jnp.cumsum(onehot, 0).astype(jnp.int32) - onehot).astype(jnp.int32)
    slot_rank = lax.optimization_barrier(jnp.sum(before * onehot, 1)).astype(jnp.int32)
    target = (flat_ids * CAP + slot_rank).astype(jnp.int32)
    sources = (jnp.arange(ROWS * TOPK, dtype=jnp.int32) // TOPK).astype(jnp.int32)
    buffer = jnp.zeros((EXPERTS * CAP, D), jnp.bfloat16).at[target].set(token_rows[sources])
    return buffer.reshape(EXPERTS, CAP, D)

def reference(patches, image_count, text_tokens, norm_gain, norm_bias, patch_proj, patch_out, merge_gain, merge_bias, merger, token_gain, router, expert_ids):
    images = patches.reshape(IMAGES, IMAGE_PATCHES, V)
    visual = lax.map(lambda image_rows: vision_image(image_rows, norm_gain, norm_bias, patch_proj, patch_out, merge_gain, merge_bias, merger), images)
    sequence = text_tokens.reshape(N_DEP, ROWS, D)
    has_image = (image_count == 1)[:, None, None]
    visual_head = jnp.where(has_image, visual, sequence[:, :VIS])
    hidden = jnp.concatenate([visual_head, sequence[:, VIS:]], 1).reshape(TOKENS, D)
    hidden_f = hidden.astype(jnp.float32)
    inv_rms = lax.rsqrt(lax.optimization_barrier(jnp.sum(hidden_f * hidden_f, -1, keepdims=True)) / D + EPS)
    scaled = hidden_f * token_gain
    logits = jnp.dot(scaled.astype(jnp.bfloat16), router, preferred_element_type=jnp.float32) * inv_rms
    normed = (scaled * inv_rms).astype(jnp.bfloat16)
    chosen = jnp.take_along_axis(logits, expert_ids, 1)
    gate_probs = jax.nn.softmax(chosen, axis=-1)
    buffers = lax.map(dispatch_rows, (normed.reshape(N_DEP, ROWS, D), expert_ids.reshape(N_DEP, ROWS, TOPK)))
    dispatched = jnp.transpose(buffers, (1, 0, 2, 3)).reshape(EXPERTS, N_DEP * CAP, D)
    return (dispatched, gate_probs)
```

```python
import math

import jax
import jax.numpy as jnp
from jax import lax
from jax.experimental import pallas as pl
from jax.experimental.pallas import tpu as pltpu
from jax.sharding import PartitionSpec as P

MESH = pl.DeviceIdType.MESH
NZ = 8
NX = 4
NY = 4
PLANE = NX * NY
SLOTS = 16
ROWS = 128

VISION_HEAD_SIZE = 72
D = 4096


EPS = 1e-06


def layer_stats_norm(values_in, gain_vec, bias_vec):
    feature_count = values_in.shape[-1]
    row_mean = jnp.sum(values_in, -1, keepdims=True) / feature_count
    row_var = (
        jnp.sum(values_in * values_in, -1, keepdims=True) / feature_count - row_mean * row_mean
    )
    return (values_in - row_mean) * lax.rsqrt(row_var + EPS) * gain_vec + bias_vec


def attend(query_rows, key_matrix, value_matrix, head_count):
    row_count = query_rows.shape[0]
    head_depth = query_rows.shape[1] // head_count
    query_per_head = query_rows.reshape(row_count, head_count, head_depth)
    key_per_head = key_matrix.reshape(key_matrix.shape[0], head_count, head_depth)
    value_per_head = value_matrix.reshape(value_matrix.shape[0], head_count, head_depth)
    attention_logits = jnp.einsum(
        "ylj,glj->lyg", query_per_head, key_per_head, preferred_element_type=jnp.float32
    ) / math.sqrt(head_depth)
    attention_weights = jax.nn.softmax(attention_logits, axis=-1).astype(jnp.bfloat16)
    attended_output = jnp.einsum(
        "irs,siy->riy", attention_weights, value_per_head, preferred_element_type=jnp.float32
    )
    return attended_output.reshape(row_count, head_count * head_depth).astype(jnp.bfloat16)


def selection(ids, first_expert):
    experts = first_expert + lax.broadcasted_iota(jnp.int32, (PLANE, ROWS), 0)
    count = jnp.zeros((PLANE, ROWS), jnp.float32)
    for k in range(ids.shape[0]):
        count += (ids[k : k + 1, :] == experts).astype(jnp.float32)
    earlier = (
        lax.broadcasted_iota(jnp.int32, (ROWS, ROWS), 0)
        < lax.broadcasted_iota(jnp.int32, (ROWS, ROWS), 1)
    ).astype(jnp.bfloat16)
    before = jnp.dot(count.astype(jnp.bfloat16), earlier, preferred_element_type=jnp.float32)
    slot = lax.broadcasted_iota(jnp.int32, (PLANE, SLOTS, ROWS), 1).astype(jnp.float32)
    first = before[:, None, :]
    last = (before + count)[:, None, :]
    chosen = (slot >= first) & (slot < last)
    return jnp.where(chosen, 1.0, 0.0).astype(jnp.bfloat16).reshape(PLANE * SLOTS, ROWS)


def dispatch_kernel(
    rows_ref, ids_ref, out_ref, held, held_ids, stage, ring_send, ring_recv, ids_send, ids_recv, out_send, out_recv
):
    dep = lax.axis_index("dep")
    z = dep // PLANE
    xy = lax.rem(dep, PLANE)
    x = xy // NY
    y = lax.rem(xy, NY)
    width = rows_ref.shape[1]
    half = width // 2

    def along_z(step):
        return {"dep": lax.rem(z + step, NZ) * PLANE + xy}

    def in_plane(step):
        to_x = lax.rem(x + step // NY, NX)
        to_y = lax.rem(y + lax.rem(step, NY), NY)
        return to_x * NY + to_y

    barrier = pltpu.get_barrier_semaphore()
    for step in range(1, NZ):
        pl.semaphore_signal(barrier, inc=1, device_id=along_z(step), device_id_type=MESH)

    def greet(step, carry):
        pl.semaphore_signal(
            barrier, inc=1, device_id={"dep": z * PLANE + in_plane(step)}, device_id_type=MESH
        )
        return carry

    lax.fori_loop(1, PLANE, greet, 0)
    pl.semaphore_wait(barrier, NZ - 1 + PLANE - 1)

    id_copies = []
    for step in range(1, NZ):
        copy = pltpu.make_async_remote_copy(
            src_ref=ids_ref,
            dst_ref=held_ids.at[NZ - step],
            send_sem=ids_send.at[step],
            recv_sem=ids_recv.at[NZ - step],
            device_id=along_z(step),
            device_id_type=MESH,
        )
        copy.start()
        id_copies.append(copy)

    def hop(number, source, slot, columns, step):
        copy = pltpu.make_async_remote_copy(
            src_ref=source.at[:, columns],
            dst_ref=held.at[slot, :, columns],
            send_sem=ring_send.at[number],
            recv_sem=ring_recv.at[number],
            device_id=along_z(step),
            device_id_type=MESH,
        )
        copy.start()
        return copy

    every = pl.ds(0, width)

    def spread(slot, source, ids):
        chosen = selection(ids, z * PLANE)
        for c in range(0, width, 512):
            stage[slot, :, c : c + 512] = jnp.dot(
                chosen, source[:, c : c + 512], preferred_element_type=jnp.float32
            ).astype(jnp.bfloat16)
        at_dest = (lax.rem(z + slot, NZ) * PLANE + xy) * SLOTS
        own = pltpu.make_async_copy(
            stage.at[slot, pl.ds(xy * SLOTS, SLOTS)], out_ref.at[pl.ds(at_dest, SLOTS)], out_recv
        )
        own.start()

        def send(step, carry):
            peer = in_plane(step)
            pltpu.make_async_remote_copy(
                src_ref=stage.at[slot, pl.ds(peer * SLOTS, SLOTS)],
                dst_ref=out_ref.at[pl.ds(at_dest, SLOTS)],
                send_sem=out_send,
                recv_sem=out_recv,
                device_id={"dep": z * PLANE + peer},
                device_id_type=MESH,
            ).start()
            return carry

        lax.fori_loop(1, PLANE, send, 0)

    right = hop(0, rows_ref, NZ - 1, every, 1)
    left = hop(4, rows_ref, 1, every, NZ - 1)
    spread(0, rows_ref, ids_ref[...])
    for step in range(1, 5):
        back, ahead = NZ - step, step
        right.wait()
        left.wait()
        if step < 3:
            right = hop(step, held.at[back], back - 1, every, 1)
            left = hop(4 + step, held.at[ahead], ahead + 1, every, NZ - 1)
        if step == 3:
            right = hop(3, held.at[back], back - 1, pl.ds(0, half), 1)
            left = hop(7, held.at[ahead], ahead + 1, pl.ds(half, half), NZ - 1)
        for slot in (back, ahead) if back != ahead else (back,):
            id_copies[NZ - 1 - slot].wait()
            spread(slot, held.at[slot], held_ids[slot])
    sent = stage.at[:, pl.ds(0, (PLANE - 1) * SLOTS)]
    pltpu.make_async_copy(sent, sent, out_send).wait()
    pltpu.make_async_copy(out_ref, out_ref, out_recv).wait()


def dispatch(normed, expert_ids):
    width = normed.shape[1]
    return pl.pallas_call(
        dispatch_kernel,
        out_shape=jax.ShapeDtypeStruct((NZ * PLANE * SLOTS, width), jnp.bfloat16),
        in_specs=[pl.BlockSpec(memory_space=pltpu.VMEM)] * 2,
        out_specs=pl.BlockSpec(memory_space=pl.ANY),
        scratch_shapes=[
            pltpu.VMEM((NZ, ROWS, width), jnp.bfloat16),
            pltpu.VMEM((NZ, 8, ROWS), jnp.int32),
            pltpu.VMEM((NZ, PLANE * SLOTS, width), jnp.bfloat16),
            pltpu.SemaphoreType.DMA((8,)),
            pltpu.SemaphoreType.DMA((8,)),
            pltpu.SemaphoreType.DMA((8,)),
            pltpu.SemaphoreType.DMA((8,)),
            pltpu.SemaphoreType.DMA,
            pltpu.SemaphoreType.DMA,
        ],
        compiler_params=pltpu.CompilerParams(
            collective_id=0, has_side_effects=True, vmem_limit_bytes=48 * 1024 * 1024
        ),
    )(normed, expert_ids.T)


def per_device(
    patches,
    image_count,
    text_tokens,
    norm_gain,
    norm_bias,
    patch_proj,
    patch_out,
    merge_gain,
    merge_bias,
    merger,
    token_gain,
    router,
    expert_ids,
):
    tp_index = lax.axis_index("tp")
    half_width = patches.shape[1]
    has_image = image_count[0] == 1
    gathered = lax.all_gather(patches, "tp", axis=1, tiled=True)
    pixels_in = gathered.astype(jnp.float32)
    normed_in = layer_stats_norm(pixels_in, norm_gain, norm_bias).astype(jnp.bfloat16)
    band_width = patch_proj.shape[2]
    projected = jnp.dot(
        normed_in,
        patch_proj.reshape(patch_proj.shape[0], 3 * band_width),
        preferred_element_type=jnp.float32,
    ).astype(jnp.bfloat16)
    query_rows = projected[:, :band_width]
    key_matrix = projected[:, band_width : 2 * band_width]
    value_matrix = projected[:, 2 * band_width :]
    attended_output = attend(query_rows, key_matrix, value_matrix, band_width // VISION_HEAD_SIZE)
    attended = lax.psum_scatter(
        jnp.dot(attended_output, patch_out, preferred_element_type=jnp.float32),
        "tp",
        scatter_dimension=1,
        tiled=True,
    )
    residual = lax.dynamic_slice_in_dim(pixels_in, tp_index * half_width, half_width, 1) + attended
    row_sums = lax.psum((jnp.sum(residual, -1), jnp.sum(residual * residual, -1)), "tp")
    full_width = 2 * half_width
    row_mean = row_sums[0] / full_width
    row_var = row_sums[1] / full_width - row_mean * row_mean
    gain_half = lax.dynamic_slice_in_dim(merge_gain, tp_index * half_width, half_width, 0)
    bias_half = lax.dynamic_slice_in_dim(merge_bias, tp_index * half_width, half_width, 0)
    merged_in = (
        (residual - row_mean[:, None]) * lax.rsqrt(row_var + EPS)[:, None] * gain_half + bias_half
    ).astype(jnp.bfloat16)
    premerge = merged_in.reshape(merged_in.shape[0] // 4, 4 * half_width)
    shard_piece = lax.all_gather(merger, "dep", axis=2, tiled=True)
    partial_terms = jnp.dot(
        premerge,
        shard_piece.reshape(4 * half_width, shard_piece.shape[2]),
        preferred_element_type=jnp.float32,
    )
    merged_rows = lax.psum_scatter(partial_terms, "tp", scatter_dimension=1, tiled=True).astype(
        jnp.bfloat16
    )
    visual_count = merged_rows.shape[0]
    visual_head = jnp.where(has_image, merged_rows, text_tokens)
    hidden = jnp.concatenate([visual_head, text_tokens[visual_count:]], 0)
    hidden_f = hidden.astype(jnp.float32)
    scaled = hidden_f * token_gain
    partial_logits = jnp.dot(
        scaled.astype(jnp.bfloat16), router, preferred_element_type=jnp.float32
    )
    logit_sum, square_sum = lax.psum((partial_logits, jnp.sum(hidden_f * hidden_f, -1)), "tp")
    inv_rms = lax.rsqrt(square_sum / D + EPS)[:, None]
    logits = logit_sum * inv_rms
    normed = (scaled * inv_rms).astype(jnp.bfloat16)
    chosen = jnp.take_along_axis(logits, expert_ids, 1)
    gate_probs = jax.nn.softmax(chosen, axis=-1)
    dispatched = dispatch(normed, expert_ids)[None]
    return (dispatched, gate_probs)


def solution(mesh):
    return jax.shard_map(
        per_device,
        mesh=mesh,
        in_specs=(
            P("dep", "tp"),
            P("dep"),
            P("dep", "tp"),
            P(),
            P(),
            P(None, None, "tp"),
            P("tp", None),
            P(),
            P(),
            P(None, "tp", "dep"),
            P("tp"),
            P("tp", None),
            P("dep", None),
        ),
        out_specs=(P("dep", None, "tp"), P("dep", None)),
        check_vma=False,
    )
```

```python
import math

import jax
import jax.numpy as jnp
from jax import lax
from jax.experimental import pallas as pl
from jax.experimental.pallas import tpu as pltpu
from jax.sharding import PartitionSpec as P

MESH = pl.DeviceIdType.MESH
BF16 = jnp.bfloat16
F32 = jnp.float32
NZ = 8
NX = 4
NY = 4
PLANE = NX * NY
SLOTS = 16
ROWS = 128
TOPK = 8
D = 4096
QUARTER = 1024
V = 1152
HALF_V = 576
PATCHES = 512
HEADS = 4
HEAD = 72
BAND = 288
OWN_COLUMNS = 32
EPS = 1e-06
TEXT = 0
IMAGE = 1


def selection(ids, first_expert):
    experts = first_expert + lax.broadcasted_iota(jnp.int32, (PLANE, ROWS), 0)
    count = jnp.zeros((PLANE, ROWS), F32)
    for k in range(TOPK):
        count += (ids[k : k + 1, :] == experts).astype(F32)
    earlier = (
        lax.broadcasted_iota(jnp.int32, (ROWS, ROWS), 0)
        < lax.broadcasted_iota(jnp.int32, (ROWS, ROWS), 1)
    ).astype(BF16)
    before = jnp.dot(count.astype(BF16), earlier, preferred_element_type=F32)
    slot = lax.broadcasted_iota(jnp.int32, (PLANE, SLOTS, ROWS), 1).astype(F32)
    first = before[:, None, :]
    last = (before + count)[:, None, :]
    chosen = (slot >= first) & (slot < last)
    return jnp.where(chosen, 1.0, 0.0).astype(BF16).reshape(PLANE * SLOTS, ROWS)


def fused_kernel(
    image_ref,
    patches_ref,
    text_ref,
    ids_ref,
    norms_ref,
    proj_ref,
    pout_ref,
    merger_ref,
    tgain_ref,
    router_ref,
    text_out,
    image_out,
    gate_ref,
    cols,
    pix,
    normed,
    qs,
    ks,
    vs,
    ctx,
    part_send,
    part_recv,
    merged,
    merged_peer,
    merged_mine,
    acts,
    weights,
    vis_send,
    vis_recv,
    vis,
    vis_all,
    text_peer,
    ids_peer,
    held_ids,
    held,
    stage,
    parts,
    gates,
    send_sems,
    recv_sems,
    acts_recv,
    vis_all_recv,
    out_send,
    out_recv,
):
    dep = lax.axis_index("dep")
    h = lax.axis_index("tp")
    z = dep // PLANE
    xy = lax.rem(dep, PLANE)
    x = xy // NY
    y = lax.rem(xy, NY)
    pair = y // 2
    p = lax.rem(y, 2)
    outs = (text_out, image_out)

    def at(to_z, to_x, to_y):
        return to_z * PLANE + to_x * NY + to_y

    def along_z(step):
        return {"dep": at(lax.rem(z + step, NZ), x, y)}

    def along_x(step):
        return {"dep": at(z, lax.rem(x + step, NX), y)}

    def along_y(step):
        return at(z, x, lax.rem(y + step, NY))

    def in_plane(step):
        to_x = lax.rem(x + step // NY, NX)
        to_y = lax.rem(y + lax.rem(step, NY), NY)
        return to_x * NY + to_y

    other_chip = dep + 1 - 2 * p
    number = [0]

    def remote(source, target, device, arrival=None):
        n = number[0]
        number[0] += 1
        copy = pltpu.make_async_remote_copy(
            src_ref=source,
            dst_ref=target,
            send_sem=send_sems.at[n],
            recv_sem=recv_sems.at[n] if arrival is None else arrival,
            device_id=device,
            device_id_type=MESH,
        )
        copy.start()
        started.append(copy)
        return copy

    started = []

    def flag(shape):
        return jnp.full(shape, image_ref[0], jnp.int32) == 1

    row_from = lax.broadcasted_iota(jnp.int32, (PATCHES, PATCHES), 0)
    row_to = lax.broadcasted_iota(jnp.int32, (PATCHES, PATCHES), 1)
    order = jnp.where(
        row_from == 4 * lax.rem(row_to, ROWS) + row_to // ROWS, 1.0, 0.0
    ).astype(BF16)
    mine = pl.ds(pl.multiple_of(h * HALF_V, HALF_V), HALF_V)
    pix[mine, :] = jnp.dot(patches_ref[...], order, preferred_element_type=F32).astype(BF16)
    weights[:, z, x] = merger_ref[...]

    barrier = pltpu.get_barrier_semaphore()

    def greet(device):
        pl.semaphore_signal(barrier, inc=1, device_id=device, device_id_type=MESH)

    for step in range(1, NZ):
        greet(along_z(step))

    def greet_plane(step, carry):
        greet({"dep": z * PLANE + in_plane(step)})
        return carry

    lax.fori_loop(1, PLANE, greet_plane, 0)
    for step in range(NY):
        greet({"dep": along_y(step), "tp": 1 - h})
    pl.semaphore_wait(barrier, NZ - 1 + PLANE - 1 + NY)

    pix_copy = remote(pix.at[mine], pix.at[mine], {"tp": 1 - h})
    ids_copy = remote(ids_ref, ids_peer, {"dep": other_chip})
    first, second = pl.ds(0, 2), pl.ds(2, 2)
    across_x = [
        remote(merger_ref.at[first], weights.at[first, z, x], along_x(step))
        for step in range(1, NX)
    ]

    def z_hop_a(step):
        back, ahead = lax.rem(z + NZ + 1 - step, NZ), lax.rem(z + step - 1, NZ)
        right = first if step < 4 else pl.ds(0, 1)
        left = first if step < 4 else pl.ds(1, 1)
        return (
            remote(weights.at[right, back], weights.at[right, back], along_z(1)),
            remote(weights.at[left, ahead], weights.at[left, ahead], along_z(NZ - 1)),
        )

    def z_hop_b(step):
        back, ahead = lax.rem(z + NZ + 1 - step, NZ), lax.rem(z + step - 1, NZ)
        right = second if step < 4 else pl.ds(2, 1)
        left = second if step < 4 else pl.ds(3, 1)
        return (
            remote(weights.at[right, back, x], weights.at[right, back, x], along_z(1)),
            remote(weights.at[left, ahead, x], weights.at[left, ahead, x], along_z(NZ - 1)),
        )

    def x_hop_b(step):
        back, ahead = lax.rem(x + NX + 1 - step, NX), lax.rem(x + step - 1, NX)
        right = second if step < 2 else pl.ds(2, 1)
        left = second if step < 2 else pl.ds(3, 1)
        return (
            remote(weights.at[right, :, back], weights.at[right, :, back], along_x(1)),
            remote(weights.at[left, :, ahead], weights.at[left, :, ahead], along_x(NX - 1)),
        )

    def arrived(copies):
        for copy in copies:
            copy.wait_recv()

    hop_b = z_hop_b(1)
    text_columns = pl.ds(pl.multiple_of((1 - p) * QUARTER, QUARTER), QUARTER)
    my_columns = pl.ds(pl.multiple_of(p * QUARTER, QUARTER), QUARTER)
    text_copy = remote(text_ref.at[:, text_columns], text_peer, {"dep": other_chip})

    for v in range(4):
        for c in range(0, V, 128):
            row = jnp.broadcast_to(norms_ref[v : v + 1, c : c + 128], (128, 128))
            cols[v, c : c + 128, :] = row.T

    ids_copy.wait_recv()
    has = flag((TOPK, ROWS))
    held_ids[0, 0:TOPK] = jnp.where(has, ids_peer[...], ids_ref[...])
    held_ids[0, TOPK:] = jnp.where(has, ids_ref[...], ids_peer[...])
    id_copies = [
        remote(held_ids.at[0], held_ids.at[NZ - step], along_z(step)) for step in range(1, NZ)
    ]

    def layer_norm(values, gain, bias):
        mean = jnp.sum(values, 0, keepdims=True) / V
        variance = jnp.sum(values * values, 0, keepdims=True) / V - mean * mean
        return (values - mean) * lax.rsqrt(variance + EPS) * gain + bias

    pix_copy.wait_recv()
    for c in range(0, PATCHES, 128):
        normed[:, c : c + 128] = layer_norm(
            pix[:, c : c + 128].astype(F32), cols[0], cols[1]
        ).astype(BF16)
    pad = jnp.zeros((128 - HEAD, PATCHES), F32)
    queries = jnp.dot(proj_ref[0], normed[...], preferred_element_type=F32)
    for head in range(HEADS):
        part = jnp.concatenate([queries[head * HEAD : (head + 1) * HEAD], pad], 0)
        qs[head] = part.astype(BF16)
    keys = jnp.dot(proj_ref[1], normed[...], preferred_element_type=F32)
    for head in range(HEADS):
        part = jnp.concatenate([keys[head * HEAD : (head + 1) * HEAD], pad], 0)
        ks[head] = part.T.astype(BF16)
    values = jnp.dot(proj_ref[2], normed[...], preferred_element_type=F32)
    for head in range(HEADS):
        vs[head] = values[head * HEAD : (head + 1) * HEAD].astype(BF16)

    arrived(across_x)
    hop_a = z_hop_a(1)
    arrived(hop_b)
    hop_b = z_hop_b(2)

    def start_stats(phase, hidden):
        scaled = hidden * tgain_ref[:, my_columns]
        me = p * 2 + h
        parts[phase, me, :, 0:128] = jnp.dot(
            scaled.astype(BF16), router_ref[p], preferred_element_type=F32
        )
        squares = jnp.sum(hidden * hidden, 1, keepdims=True)
        parts[phase, me, :, 128:256] = jnp.broadcast_to(squares, (ROWS, 128))
        return [
            remote(
                parts.at[phase, me],
                parts.at[phase, me],
                {"dep": dep if dp == 0 else other_chip, "tp": h if dh == 0 else 1 - h},
            )
            for dp, dh in ((0, 1), (1, 0), (1, 1))
        ]

    def normalise(phase, hidden):
        total = parts[phase, 0] + parts[phase, 1] + parts[phase, 2] + parts[phase, 3]
        inv_rms = lax.rsqrt(total[:, 128:129] / D + EPS)
        held[phase, 0] = (hidden * tgain_ref[:, my_columns] * inv_rms).astype(BF16)
        return total

    def gate(phase, total):
        logits = total[:, 0:128].T
        squares = total[:, 128:256].T
        logits = logits * lax.rsqrt(squares[0:1, :] / D + EPS)
        expert = lax.broadcasted_iota(jnp.int32, (128, ROWS), 0)
        ids = held_ids[0, phase * TOPK : (phase + 1) * TOPK]
        for k in range(TOPK):
            gates[phase, k : k + 1, :] = jnp.sum(
                jnp.where(ids[k : k + 1, :] == expert, logits, 0.0), 0, keepdims=True
            )
        chosen = gates[phase]
        raised = jnp.exp(chosen - jnp.max(chosen, 0, keepdims=True))
        return raised / jnp.sum(raised, 0, keepdims=True)

    def ring_hop(phase, step):
        back, ahead = lax.rem(NZ + 1 - step, NZ), step - 1
        right = pl.ds(0, QUARTER if step < 4 else QUARTER // 2)
        left = right if step < 4 else pl.ds(QUARTER // 2, QUARTER // 2)
        return (
            remote(
                held.at[phase, back, :, right], held.at[phase, NZ - step, :, right], along_z(1)
            ),
            remote(
                held.at[phase, ahead, :, left], held.at[phase, step, :, left], along_z(NZ - 1)
            ),
        )

    def spread(phase, slot):
        ids = held_ids[slot, phase * TOPK : (phase + 1) * TOPK]
        chosen = selection(ids, z * PLANE)
        for c in range(0, QUARTER, 512):
            stage[phase, slot, :, c : c + 512] = jnp.dot(
                chosen, held[phase, slot, :, c : c + 512], preferred_element_type=F32
            ).astype(BF16)
        source_pair = lax.rem(z + slot, NZ) * (PLANE // 2) + xy // 2
        at_dest = outs[phase].at[pl.ds(source_pair * SLOTS, SLOTS), my_columns]
        pltpu.make_async_copy(
            stage.at[phase, slot, pl.ds(xy * SLOTS, SLOTS)], at_dest, out_recv.at[phase]
        ).start()

        def send(step, carry):
            peer = in_plane(step)
            pltpu.make_async_remote_copy(
                src_ref=stage.at[phase, slot, pl.ds(peer * SLOTS, SLOTS)],
                dst_ref=at_dest,
                send_sem=out_send.at[phase],
                recv_sem=out_recv.at[phase],
                device_id={"dep": z * PLANE + peer},
                device_id_type=MESH,
            ).start()
            return carry

        lax.fori_loop(1, PLANE, send, 0)

    text_copy.wait_recv()

    def text_hidden():
        return jnp.where(
            flag((ROWS, QUARTER)),
            text_peer[...].astype(F32),
            text_ref[:, my_columns].astype(F32),
        )

    text_stats = start_stats(TEXT, text_hidden())

    def attend(lanes):
        for head in range(HEADS):
            scores = jnp.dot(ks[head], qs[head, :, lanes], preferred_element_type=F32)
            scores = scores * (1.0 / math.sqrt(HEAD))
            raised = jnp.exp(scores - jnp.max(scores, 0, keepdims=True))
            probs = raised * (1.0 / jnp.sum(raised, 0, keepdims=True))
            ctx[head * HEAD : (head + 1) * HEAD, :] = jnp.dot(
                vs[head], probs.astype(BF16), preferred_element_type=F32
            )
        return ctx[...].astype(BF16)

    def out_product(context, lo):
        return lax.dot_general(
            pout_ref[:, lo : lo + 384],
            context,
            (((0,), (0,)), ((), ())),
            preferred_element_type=F32,
        )

    my_rows = pl.ds(pl.multiple_of(h * 256, 256), 256)
    their_rows = pl.ds(pl.multiple_of((1 - h) * 256, 256), 256)
    context = attend(their_rows)
    part_copies = []
    for lo in range(0, V, 384):
        part_send[lo : lo + 384, :] = out_product(context, lo)
        block = pl.ds(lo, 384)
        part_copies.append(remote(part_send.at[block], part_recv.at[block], {"tp": 1 - h}))

    arrived(hop_b)
    hop_b = z_hop_b(3)
    arrived(text_stats)
    text_total = normalise(TEXT, text_hidden())
    ring = ring_hop(TEXT, 1)
    spread(TEXT, 0)

    context = attend(my_rows)
    arrived(hop_b)
    hop_b = z_hop_b(4)
    arrived(hop_a)
    hop_a = z_hop_a(2)
    arrived(part_copies)
    for lo in range(0, V, 384):
        block = pl.ds(lo, 384)
        part_recv[block, :] += out_product(context, lo) + pix[block, my_rows].astype(F32)
    for c in range(0, 256, 128):
        merged[:, c : c + 128] = layer_norm(part_recv[:, c : c + 128], cols[2], cols[3]).astype(
            BF16
        )
    keep = pl.ds(pl.multiple_of(p * 128, 128), 128)
    give = pl.ds(pl.multiple_of((1 - p) * 128, 128), 128)
    merged_copy = remote(merged.at[:, give], merged_peer, {"dep": other_chip})

    arrived(hop_b)
    hop_b = x_hop_b(1)
    arrived(ring)
    ring = ring_hop(TEXT, 2)
    for slot in (1, 7):
        id_copies[NZ - 1 - slot].wait_recv()
        spread(TEXT, slot)
    merged_copy.wait_recv()
    merged_mine[...] = jnp.where(
        flag((V, 128)), merged[:, keep].astype(F32), merged_peer[...].astype(F32)
    ).astype(BF16)
    place = 2 * h + p
    lanes = pl.ds(pl.multiple_of(pair * 128, 128), 128)
    own_half = merged_mine.at[mine]
    theirs = merged_mine.at[pl.ds(pl.multiple_of((1 - h) * HALF_V, HALF_V), HALF_V)]
    pltpu.make_async_copy(own_half, acts.at[place, :, lanes], acts_recv).start()
    for step in range(NY):
        if step > 0:
            remote(own_half, acts.at[place, :, lanes], {"dep": along_y(step)}, acts_recv)
        remote(
            theirs, acts.at[place, :, lanes], {"dep": along_y(step), "tp": 1 - h}, acts_recv
        )

    arrived(hop_a)
    hop_a = z_hop_a(3)
    arrived(ring)
    ring = ring_hop(TEXT, 3)
    for slot in (2, 6):
        id_copies[NZ - 1 - slot].wait_recv()
        spread(TEXT, slot)
    arrived(ring)
    ring = ring_hop(TEXT, 4)
    for slot in (3, 5):
        id_copies[NZ - 1 - slot].wait_recv()
        spread(TEXT, slot)
    arrived(hop_a)
    hop_a = z_hop_a(4)
    arrived(hop_b)
    hop_b = x_hop_b(2)
    arrived(ring)
    id_copies[NZ - 1 - 4].wait_recv()
    spread(TEXT, 4)
    text_gate = gate(TEXT, text_total)
    arrived(hop_a)
    arrived(hop_b)
    pltpu.make_async_copy(acts, acts, acts_recv).wait()

    def columns_of(zs):
        total = None
        for i in range(4):
            block = weights[i, pl.ds(zs, 2)].reshape(2 * NX * OWN_COLUMNS, HALF_V)
            product = jnp.dot(block, acts[i], preferred_element_type=F32)
            total = product if total is None else total + product
        return total

    vis_copies = []
    for c in range(2):
        vis_send[c] = columns_of((1 - h) * 4 + 2 * c)
        vis_copies.append(remote(vis_send.at[c], vis_recv.at[c], {"tp": 1 - h}))
    for c in range(2):
        product = columns_of(h * 4 + 2 * c)
        vis_copies[c].wait_recv()
        vis[pl.ds(8 * c, 8)] = (product + vis_recv[c]).astype(BF16).reshape(8, OWN_COLUMNS, 256)

    def vis_block(to_y):
        return vis.at[
            pl.ds(lax.rem(to_y, 2) * 8, 8), :, pl.ds(pl.multiple_of((to_y // 2) * 128, 128), 128)
        ]

    pltpu.make_async_copy(vis_block(y), vis_all.at[:, y], vis_all_recv).start()
    for step in range(1, NY):
        to_y = lax.rem(y + step, NY)
        remote(vis_block(to_y), vis_all.at[:, y], {"dep": along_y(step)}, vis_all_recv)
    pltpu.make_async_copy(vis_all, vis_all, vis_all_recv).wait()

    def image_hidden():
        return vis_all[...].reshape(QUARTER, ROWS).astype(F32).T

    image_stats = start_stats(IMAGE, image_hidden())
    arrived(image_stats)
    image_total = normalise(IMAGE, image_hidden())
    ring = ring_hop(IMAGE, 1)
    spread(IMAGE, 0)
    image_gate = gate(IMAGE, image_total)
    gate_ref[...] = jnp.where(flag((TOPK, ROWS)), image_gate, text_gate)
    for step in range(1, 5):
        arrived(ring)
        if step < 4:
            ring = ring_hop(IMAGE, step + 1)
        for slot in (step, NZ - step) if step < 4 else (4,):
            spread(IMAGE, slot)

    for copy in started:
        copy.wait_send()
    for phase in (TEXT, IMAGE):
        sent = stage.at[phase, :, pl.ds(0, (PLANE - 1) * SLOTS)]
        pltpu.make_async_copy(sent, sent, out_send.at[phase]).wait()
        pltpu.make_async_copy(outs[phase], outs[phase], out_recv.at[phase]).wait()


def fused(image_count, patches, text, ids, norms, proj, pout, merger, tgain, router):
    vmem = pl.BlockSpec(memory_space=pltpu.VMEM)
    rows = NZ * PLANE // 2 * SLOTS
    buffer = jax.ShapeDtypeStruct((rows, 2 * QUARTER), BF16)
    copies = 96
    return pl.pallas_call(
        fused_kernel,
        out_shape=(buffer, buffer, jax.ShapeDtypeStruct((TOPK, ROWS), F32)),
        in_specs=[pl.BlockSpec(memory_space=pltpu.SMEM)] + [vmem] * 9,
        out_specs=(
            pl.BlockSpec(memory_space=pl.ANY),
            pl.BlockSpec(memory_space=pl.ANY),
            vmem,
        ),
        scratch_shapes=[
            pltpu.VMEM((4, V, 128), F32),
            pltpu.VMEM((V, PATCHES), BF16),
            pltpu.VMEM((V, PATCHES), BF16),
            pltpu.VMEM((HEADS, 128, PATCHES), BF16),
            pltpu.VMEM((HEADS, PATCHES, 128), BF16),
            pltpu.VMEM((HEADS, HEAD, PATCHES), BF16),
            pltpu.VMEM((BAND, 256), F32),
            pltpu.VMEM((V, 256), F32),
            pltpu.VMEM((V, 256), F32),
            pltpu.VMEM((V, 256), BF16),
            pltpu.VMEM((V, 128), BF16),
            pltpu.VMEM((V, 128), BF16),
            pltpu.VMEM((4, HALF_V, 256), BF16),
            pltpu.VMEM((4, NZ, NX, OWN_COLUMNS, HALF_V), BF16),
            pltpu.VMEM((2, 256, 256), F32),
            pltpu.VMEM((2, 256, 256), F32),
            pltpu.VMEM((16, OWN_COLUMNS, 256), BF16),
            pltpu.VMEM((8, NY, OWN_COLUMNS, ROWS), BF16),
            pltpu.VMEM((ROWS, QUARTER), BF16),
            pltpu.VMEM((TOPK, ROWS), jnp.int32),
            pltpu.VMEM((NZ, 2 * TOPK, ROWS), jnp.int32),
            pltpu.VMEM((2, NZ, ROWS, QUARTER), BF16),
            pltpu.VMEM((2, NZ, PLANE * SLOTS, QUARTER), BF16),
            pltpu.VMEM((2, 4, ROWS, 256), F32),
            pltpu.VMEM((2, TOPK, ROWS), F32),
            pltpu.SemaphoreType.DMA((copies,)),
            pltpu.SemaphoreType.DMA((copies,)),
            pltpu.SemaphoreType.DMA,
            pltpu.SemaphoreType.DMA,
            pltpu.SemaphoreType.DMA((2,)),
            pltpu.SemaphoreType.DMA((2,)),
        ],
        compiler_params=pltpu.CompilerParams(
            collective_id=0, has_side_effects=True, vmem_limit_bytes=56 * 1024 * 1024
        ),
    )(image_count, patches, text, ids, norms, proj, pout, merger, tgain, router)


def interleave_kernel(counts_ref, text_ref, image_ref, out_ref, sem):
    def pair_rows(ref, k):
        return ref.at[pl.ds(pl.multiple_of(k * SLOTS, SLOTS), SLOTS)]

    def step(k, carry):
        first = counts_ref[2 * k]
        pltpu.make_async_copy(pair_rows(text_ref, k), pair_rows(out_ref, 2 * k + first), sem).start()
        pltpu.make_async_copy(
            pair_rows(image_ref, k), pair_rows(out_ref, 2 * k + 1 - first), sem
        ).start()
        return carry

    lax.fori_loop(0, counts_ref.shape[0] // 2, step, 0)
    pltpu.make_async_copy(out_ref, out_ref, sem).wait()


def interleave(counts, text_rows, image_rows):
    return pl.pallas_call(
        interleave_kernel,
        out_shape=jax.ShapeDtypeStruct((2 * text_rows.shape[0], text_rows.shape[1]), BF16),
        in_specs=[
            pl.BlockSpec(memory_space=pltpu.SMEM),
            pl.BlockSpec(memory_space=pl.ANY),
            pl.BlockSpec(memory_space=pl.ANY),
        ],
        out_specs=pl.BlockSpec(memory_space=pl.ANY),
        scratch_shapes=[pltpu.SemaphoreType.DMA],
    )(counts, text_rows, image_rows)


def per_device(
    patches,
    image_count,
    text_tokens,
    norm_gain,
    norm_bias,
    patch_proj,
    patch_out,
    merge_gain,
    merge_bias,
    merger,
    token_gain,
    router,
    expert_ids,
):
    counts = lax.all_gather(image_count, "dep", axis=0, tiled=True)
    text_rows, image_rows, gates = fused(
        image_count,
        patches.T,
        text_tokens,
        expert_ids.T,
        jnp.stack([norm_gain, norm_bias, merge_gain, merge_bias]),
        patch_proj.transpose(1, 2, 0),
        patch_out,
        merger.transpose(0, 2, 1),
        token_gain[None],
        router.reshape(2, QUARTER, router.shape[1]),
    )
    return interleave(counts, text_rows, image_rows)[None], gates.T


def solution(mesh):
    return jax.shard_map(
        per_device,
        mesh=mesh,
        in_specs=(
            P("dep", "tp"),
            P("dep"),
            P("dep", "tp"),
            P(),
            P(),
            P(None, None, "tp"),
            P("tp", None),
            P(),
            P(),
            P(None, "tp", "dep"),
            P("tp"),
            P("tp", None),
            P("dep", None),
        ),
        out_specs=(P("dep", None, "tp"), P("dep", None)),
        check_vma=False,
    )
```

```python
import math

import jax
import jax.numpy as jnp
from jax import lax
from jax.experimental import pallas as pl
from jax.experimental.pallas import tpu as pltpu
from jax.sharding import PartitionSpec as P

MESH = pl.DeviceIdType.MESH
BF16 = jnp.bfloat16
F32 = jnp.float32
NZ = 8
NX = 4
NY = 4
PLANE = NX * NY
SLOTS = 16
ROWS = 128
TOPK = 8
D = 4096
QUARTER = 1024
V = 1152
HALF_V = 576
PATCHES = 512
HEADS = 4
HEAD = 72
BAND = 288
OWN_COLUMNS = 32
EPS = 1e-06
TEXT = 0
IMAGE = 1


def selection(ids, first_expert):
    experts = first_expert + lax.broadcasted_iota(jnp.int32, (PLANE, ROWS), 0)
    count = jnp.zeros((PLANE, ROWS), F32)
    for k in range(TOPK):
        count += (ids[k : k + 1, :] == experts).astype(F32)
    earlier = (
        lax.broadcasted_iota(jnp.int32, (ROWS, ROWS), 0)
        < lax.broadcasted_iota(jnp.int32, (ROWS, ROWS), 1)
    ).astype(BF16)
    before = jnp.dot(count.astype(BF16), earlier, preferred_element_type=F32)
    slot = lax.broadcasted_iota(jnp.int32, (PLANE, SLOTS, ROWS), 1).astype(F32)
    first = before[:, None, :]
    last = (before + count)[:, None, :]
    chosen = (slot >= first) & (slot < last)
    return jnp.where(chosen, 1.0, 0.0).astype(BF16).reshape(PLANE * SLOTS, ROWS)


def fused_kernel(
    image_ref,
    patches_ref,
    text_ref,
    ids_ref,
    norm_gain_ref,
    norm_bias_ref,
    merge_gain_ref,
    merge_bias_ref,
    proj_ref,
    pout_ref,
    merger_ref,
    tgain_ref,
    router_ref,
    text_out,
    image_out,
    gate_ref,
    counts_ref,
    cols,
    pix,
    normed,
    qs,
    ks,
    vs,
    ctx,
    part_send,
    part_recv,
    merged,
    merged_peer,
    merged_mine,
    acts,
    weights,
    vis_send,
    vis_recv,
    vis,
    vis_all,
    text_peer,
    ids_peer,
    held_ids,
    plane_counts,
    all_counts,
    held,
    stage,
    parts,
    gates,
    send_sems,
    recv_sems,
    acts_recv,
    vis_all_recv,
    out_send,
    out_recv,
    counts_send,
    counts_recv,
):
    dep = lax.axis_index("dep")
    h = lax.axis_index("tp")
    z = dep // PLANE
    xy = lax.rem(dep, PLANE)
    x = xy // NY
    y = lax.rem(xy, NY)
    pair = y // 2
    p = lax.rem(y, 2)
    outs = (text_out, image_out)

    def at(to_z, to_x, to_y):
        return to_z * PLANE + to_x * NY + to_y

    def along_z(step):
        return {"dep": at(lax.rem(z + step, NZ), x, y)}

    def along_x(step):
        return {"dep": at(z, lax.rem(x + step, NX), y)}

    def along_y(step):
        return at(z, x, lax.rem(y + step, NY))

    def in_plane(step):
        to_x = lax.rem(x + step // NY, NX)
        to_y = lax.rem(y + lax.rem(step, NY), NY)
        return to_x * NY + to_y

    other_chip = dep + 1 - 2 * p
    number = [0]

    def remote(source, target, device, arrival=None):
        n = number[0]
        number[0] += 1
        copy = pltpu.make_async_remote_copy(
            src_ref=source,
            dst_ref=target,
            send_sem=send_sems.at[n],
            recv_sem=recv_sems.at[n] if arrival is None else arrival,
            device_id=device,
            device_id_type=MESH,
        )
        copy.start()
        started.append(copy)
        return copy

    started = []

    def flag(shape):
        return jnp.full(shape, image_ref[0], jnp.int32) == 1

    row_from = lax.broadcasted_iota(jnp.int32, (PATCHES, PATCHES), 0)
    row_to = lax.broadcasted_iota(jnp.int32, (PATCHES, PATCHES), 1)
    order = jnp.where(
        row_from == 4 * lax.rem(row_to, ROWS) + row_to // ROWS, 1.0, 0.0
    ).astype(BF16)
    mine = pl.ds(pl.multiple_of(h * HALF_V, HALF_V), HALF_V)
    pix[mine, :] = jnp.dot(patches_ref[...], order, preferred_element_type=F32).astype(BF16)
    weights[:, z, x] = merger_ref[...]

    barrier = pltpu.get_barrier_semaphore()

    def greet(device):
        pl.semaphore_signal(barrier, inc=1, device_id=device, device_id_type=MESH)

    for step in range(1, NZ):
        greet(along_z(step))

    def greet_plane(step, carry):
        greet({"dep": z * PLANE + in_plane(step)})
        return carry

    lax.fori_loop(1, PLANE, greet_plane, 0)
    for step in range(NY):
        greet({"dep": along_y(step), "tp": 1 - h})
    pl.semaphore_wait(barrier, NZ - 1 + PLANE - 1 + NY)

    pix_copy = remote(pix.at[mine], pix.at[mine], {"tp": 1 - h})
    ids_copy = remote(ids_ref, ids_peer, {"dep": other_chip})
    first, second = pl.ds(0, 2), pl.ds(2, 2)
    across_x = [
        remote(merger_ref.at[first], weights.at[first, z, x], along_x(step))
        for step in range(1, NX)
    ]

    def z_hop_a(step):
        back, ahead = lax.rem(z + NZ + 1 - step, NZ), lax.rem(z + step - 1, NZ)
        right = first if step < 4 else pl.ds(0, 1)
        left = first if step < 4 else pl.ds(1, 1)
        return (
            remote(weights.at[right, back], weights.at[right, back], along_z(1)),
            remote(weights.at[left, ahead], weights.at[left, ahead], along_z(NZ - 1)),
        )

    def z_hop_b(step):
        back, ahead = lax.rem(z + NZ + 1 - step, NZ), lax.rem(z + step - 1, NZ)
        right = second if step < 4 else pl.ds(2, 1)
        left = second if step < 4 else pl.ds(3, 1)
        return (
            remote(weights.at[right, back, x], weights.at[right, back, x], along_z(1)),
            remote(weights.at[left, ahead, x], weights.at[left, ahead, x], along_z(NZ - 1)),
        )

    def x_hop_b(step):
        back, ahead = lax.rem(x + NX + 1 - step, NX), lax.rem(x + step - 1, NX)
        right = second if step < 2 else pl.ds(2, 1)
        left = second if step < 2 else pl.ds(3, 1)
        return (
            remote(weights.at[right, :, back], weights.at[right, :, back], along_x(1)),
            remote(weights.at[left, :, ahead], weights.at[left, :, ahead], along_x(NX - 1)),
        )

    def arrived(copies):
        for copy in copies:
            copy.wait_recv()

    hop_b = z_hop_b(1)
    text_columns = pl.ds(pl.multiple_of((1 - p) * QUARTER, QUARTER), QUARTER)
    my_columns = pl.ds(pl.multiple_of(p * QUARTER, QUARTER), QUARTER)
    text_copy = remote(text_ref.at[:, text_columns], text_peer, {"dep": other_chip})

    for v, vector in enumerate((norm_gain_ref, norm_bias_ref, merge_gain_ref, merge_bias_ref)):
        for c in range(0, V, 128):
            row = jnp.broadcast_to(vector[c : c + 128].reshape(1, 128), (128, 128))
            cols[v, c : c + 128, :] = row.T

    ids_copy.wait_recv()
    has = flag((TOPK, ROWS))
    held_ids[0, 0:TOPK] = jnp.where(has, ids_peer[...], ids_ref[...])
    held_ids[0, TOPK : 2 * TOPK] = jnp.where(has, ids_ref[...], ids_peer[...])
    held_ids[0, 2 * TOPK :] = jnp.full((8, ROWS), image_ref[0], jnp.int32)
    id_copies = [
        remote(held_ids.at[0], held_ids.at[NZ - step], along_z(step)) for step in range(1, NZ)
    ]

    def layer_norm(values, gain, bias):
        mean = jnp.sum(values, 0, keepdims=True) / V
        variance = jnp.sum(values * values, 0, keepdims=True) / V - mean * mean
        return (values - mean) * lax.rsqrt(variance + EPS) * gain + bias

    pix_copy.wait_recv()
    for c in range(0, PATCHES, 128):
        normed[:, c : c + 128] = layer_norm(
            pix[:, c : c + 128].astype(F32), cols[0], cols[1]
        ).astype(BF16)
    pad = jnp.zeros((128 - HEAD, PATCHES), F32)
    queries = jnp.dot(proj_ref[0], normed[...], preferred_element_type=F32)
    for head in range(HEADS):
        part = jnp.concatenate([queries[head * HEAD : (head + 1) * HEAD], pad], 0)
        qs[head] = part.astype(BF16)
    keys = jnp.dot(proj_ref[1], normed[...], preferred_element_type=F32)
    for head in range(HEADS):
        part = jnp.concatenate([keys[head * HEAD : (head + 1) * HEAD], pad], 0)
        ks[head] = part.T.astype(BF16)
    values = jnp.dot(proj_ref[2], normed[...], preferred_element_type=F32)
    for head in range(HEADS):
        vs[head] = values[head * HEAD : (head + 1) * HEAD].astype(BF16)

    arrived(across_x)
    hop_a = z_hop_a(1)
    arrived(hop_b)
    hop_b = z_hop_b(2)

    def start_stats(phase, hidden):
        scaled = hidden * tgain_ref[my_columns].reshape(1, QUARTER)
        me = p * 2 + h
        parts[phase, me, :, 0:128] = jnp.dot(
            scaled.astype(BF16), router_ref[p], preferred_element_type=F32
        )
        squares = jnp.sum(hidden * hidden, 1, keepdims=True)
        parts[phase, me, :, 128:256] = jnp.broadcast_to(squares, (ROWS, 128))
        return [
            remote(
                parts.at[phase, me],
                parts.at[phase, me],
                {"dep": dep if dp == 0 else other_chip, "tp": h if dh == 0 else 1 - h},
            )
            for dp, dh in ((0, 1), (1, 0), (1, 1))
        ]

    def normalise(phase, hidden):
        total = parts[phase, 0] + parts[phase, 1] + parts[phase, 2] + parts[phase, 3]
        inv_rms = lax.rsqrt(total[:, 128:129] / D + EPS)
        held[phase, 0] = (hidden * tgain_ref[my_columns].reshape(1, QUARTER) * inv_rms).astype(BF16)
        return total

    def gate(phase, total):
        logits = total[:, 0:128].T
        squares = total[:, 128:256].T
        logits = logits * lax.rsqrt(squares[0:1, :] / D + EPS)
        expert = lax.broadcasted_iota(jnp.int32, (128, ROWS), 0)
        ids = held_ids[0, phase * TOPK : (phase + 1) * TOPK]
        for k in range(TOPK):
            gates[phase, k : k + 1, :] = jnp.sum(
                jnp.where(ids[k : k + 1, :] == expert, logits, 0.0), 0, keepdims=True
            )
        chosen = gates[phase]
        raised = jnp.exp(chosen - jnp.max(chosen, 0, keepdims=True))
        return raised / jnp.sum(raised, 0, keepdims=True)

    def ring_hop(phase, step):
        back, ahead = lax.rem(NZ + 1 - step, NZ), step - 1
        right = pl.ds(0, QUARTER if step < 4 else QUARTER // 2)
        left = right if step < 4 else pl.ds(QUARTER // 2, QUARTER // 2)
        return (
            remote(
                held.at[phase, back, :, right], held.at[phase, NZ - step, :, right], along_z(1)
            ),
            remote(
                held.at[phase, ahead, :, left], held.at[phase, step, :, left], along_z(NZ - 1)
            ),
        )

    def spread(phase, slot):
        ids = held_ids[slot, phase * TOPK : (phase + 1) * TOPK]
        chosen = selection(ids, z * PLANE)
        for c in range(0, QUARTER, 512):
            stage[phase, slot, :, c : c + 512] = jnp.dot(
                chosen, held[phase, slot, :, c : c + 512], preferred_element_type=F32
            ).astype(BF16)
        source_pair = lax.rem(z + slot, NZ) * (PLANE // 2) + xy // 2
        at_dest = outs[phase].at[pl.ds(source_pair * SLOTS, SLOTS), my_columns]
        pltpu.make_async_copy(
            stage.at[phase, slot, pl.ds(xy * SLOTS, SLOTS)], at_dest, out_recv.at[phase]
        ).start()

        def send(step, carry):
            peer = in_plane(step)
            pltpu.make_async_remote_copy(
                src_ref=stage.at[phase, slot, pl.ds(peer * SLOTS, SLOTS)],
                dst_ref=at_dest,
                send_sem=out_send.at[phase],
                recv_sem=out_recv.at[phase],
                device_id={"dep": z * PLANE + peer},
                device_id_type=MESH,
            ).start()
            return carry

        lax.fori_loop(1, PLANE, send, 0)

    text_copy.wait_recv()

    def text_hidden():
        return jnp.where(
            flag((ROWS, QUARTER)),
            text_peer[...].astype(F32),
            text_ref[:, my_columns].astype(F32),
        )

    text_stats = start_stats(TEXT, text_hidden())

    def attend(lanes):
        for head in range(HEADS):
            scores = jnp.dot(ks[head], qs[head, :, lanes], preferred_element_type=F32)
            scores = scores * (1.0 / math.sqrt(HEAD))
            raised = jnp.exp(scores - jnp.max(scores, 0, keepdims=True))
            probs = raised * (1.0 / jnp.sum(raised, 0, keepdims=True))
            ctx[head * HEAD : (head + 1) * HEAD, :] = jnp.dot(
                vs[head], probs.astype(BF16), preferred_element_type=F32
            )
        return ctx[...].astype(BF16)

    def out_product(context, lo):
        return lax.dot_general(
            pout_ref[:, lo : lo + 384],
            context,
            (((0,), (0,)), ((), ())),
            preferred_element_type=F32,
        )

    my_rows = pl.ds(pl.multiple_of(h * 256, 256), 256)
    their_rows = pl.ds(pl.multiple_of((1 - h) * 256, 256), 256)
    context = attend(their_rows)
    part_copies = []
    for lo in range(0, V, 384):
        part_send[lo : lo + 384, :] = out_product(context, lo)
        block = pl.ds(lo, 384)
        part_copies.append(remote(part_send.at[block], part_recv.at[block], {"tp": 1 - h}))

    arrived(hop_b)
    hop_b = z_hop_b(3)
    arrived(text_stats)
    text_total = normalise(TEXT, text_hidden())
    ring = ring_hop(TEXT, 1)
    spread(TEXT, 0)

    context = attend(my_rows)
    arrived(hop_b)
    hop_b = z_hop_b(4)
    arrived(hop_a)
    hop_a = z_hop_a(2)
    arrived(part_copies)
    for lo in range(0, V, 384):
        block = pl.ds(lo, 384)
        part_recv[block, :] += out_product(context, lo) + pix[block, my_rows].astype(F32)
    for c in range(0, 256, 128):
        merged[:, c : c + 128] = layer_norm(part_recv[:, c : c + 128], cols[2], cols[3]).astype(
            BF16
        )
    keep = pl.ds(pl.multiple_of(p * 128, 128), 128)
    give = pl.ds(pl.multiple_of((1 - p) * 128, 128), 128)
    merged_copy = remote(merged.at[:, give], merged_peer, {"dep": other_chip})

    arrived(hop_b)
    hop_b = x_hop_b(1)
    arrived(ring)
    ring = ring_hop(TEXT, 2)
    for slot in (1, 7):
        id_copies[NZ - 1 - slot].wait_recv()
        spread(TEXT, slot)
    merged_copy.wait_recv()
    merged_mine[...] = jnp.where(
        flag((V, 128)), merged[:, keep].astype(F32), merged_peer[...].astype(F32)
    ).astype(BF16)
    place = 2 * h + p
    lanes = pl.ds(pl.multiple_of(pair * 128, 128), 128)
    own_half = merged_mine.at[mine]
    theirs = merged_mine.at[pl.ds(pl.multiple_of((1 - h) * HALF_V, HALF_V), HALF_V)]
    pltpu.make_async_copy(own_half, acts.at[place, :, lanes], acts_recv).start()
    for step in range(NY):
        if step > 0:
            remote(own_half, acts.at[place, :, lanes], {"dep": along_y(step)}, acts_recv)
        remote(
            theirs, acts.at[place, :, lanes], {"dep": along_y(step), "tp": 1 - h}, acts_recv
        )

    arrived(hop_a)
    hop_a = z_hop_a(3)
    arrived(ring)
    ring = ring_hop(TEXT, 3)
    for slot in (2, 6):
        id_copies[NZ - 1 - slot].wait_recv()
        spread(TEXT, slot)
    arrived(ring)
    ring = ring_hop(TEXT, 4)
    for slot in (3, 5):
        id_copies[NZ - 1 - slot].wait_recv()
        spread(TEXT, slot)
    arrived(hop_a)
    hop_a = z_hop_a(4)
    arrived(hop_b)
    hop_b = x_hop_b(2)
    arrived(ring)
    id_copies[NZ - 1 - 4].wait_recv()
    spread(TEXT, 4)
    text_gate = gate(TEXT, text_total)
    for slot in range(NZ):
        plane_counts[pl.ds(lax.rem(z + slot, NZ), 1), :] = held_ids[slot, 2 * TOPK : 2 * TOPK + 1]
    all_counts[xy] = plane_counts[...]

    def send_counts(step, carry):
        pltpu.make_async_remote_copy(
            src_ref=plane_counts,
            dst_ref=all_counts.at[xy],
            send_sem=counts_send,
            recv_sem=counts_recv,
            device_id={"dep": z * PLANE + in_plane(step)},
            device_id_type=MESH,
        ).start()
        return carry

    lax.fori_loop(1, PLANE, send_counts, 0)
    arrived(hop_a)
    arrived(hop_b)
    pltpu.make_async_copy(acts, acts, acts_recv).wait()

    def columns_of(zs):
        total = None
        for i in range(4):
            block = weights[i, pl.ds(zs, 2)].reshape(2 * NX * OWN_COLUMNS, HALF_V)
            product = jnp.dot(block, acts[i], preferred_element_type=F32)
            total = product if total is None else total + product
        return total

    vis_copies = []
    for c in range(2):
        vis_send[c] = columns_of((1 - h) * 4 + 2 * c)
        vis_copies.append(remote(vis_send.at[c], vis_recv.at[c], {"tp": 1 - h}))
    for c in range(2):
        product = columns_of(h * 4 + 2 * c)
        vis_copies[c].wait_recv()
        vis[pl.ds(8 * c, 8)] = (product + vis_recv[c]).astype(BF16).reshape(8, OWN_COLUMNS, 256)

    def vis_block(to_y):
        return vis.at[
            pl.ds(lax.rem(to_y, 2) * 8, 8), :, pl.ds(pl.multiple_of((to_y // 2) * 128, 128), 128)
        ]

    pltpu.make_async_copy(vis_block(y), vis_all.at[:, y], vis_all_recv).start()
    for step in range(1, NY):
        to_y = lax.rem(y + step, NY)
        remote(vis_block(to_y), vis_all.at[:, y], {"dep": along_y(step)}, vis_all_recv)
    pltpu.make_async_copy(vis_all, vis_all, vis_all_recv).wait()

    def image_hidden():
        return vis_all[...].reshape(QUARTER, ROWS).astype(F32).T

    image_stats = start_stats(IMAGE, image_hidden())
    arrived(image_stats)
    image_total = normalise(IMAGE, image_hidden())
    ring = ring_hop(IMAGE, 1)
    spread(IMAGE, 0)
    image_gate = gate(IMAGE, image_total)
    gate_ref[...] = jnp.where(flag((TOPK, ROWS)), image_gate, text_gate)
    for step in range(1, 5):
        arrived(ring)
        if step < 4:
            ring = ring_hop(IMAGE, step + 1)
        for slot in (step, NZ - step) if step < 4 else (4,):
            spread(IMAGE, slot)

    for copy in started:
        copy.wait_send()
    others = all_counts.at[pl.ds(0, PLANE - 1)]
    pltpu.make_async_copy(others, others, counts_send).wait()
    pltpu.make_async_copy(others, others, counts_recv).wait()
    lane = lax.broadcasted_iota(jnp.int32, (NZ, ROWS), 1)
    total_counts = jnp.zeros((NZ, ROWS), jnp.int32)
    for source in range(PLANE):
        total_counts += jnp.where(lane == source, all_counts[source], 0)
    counts_ref[...] = total_counts
    for phase in (TEXT, IMAGE):
        sent = stage.at[phase, :, pl.ds(0, (PLANE - 1) * SLOTS)]
        pltpu.make_async_copy(sent, sent, out_send.at[phase]).wait()
        pltpu.make_async_copy(outs[phase], outs[phase], out_recv.at[phase]).wait()


def fused(image_count, patches, text, ids, norms, proj, pout, merger, tgain, router):
    vmem = pl.BlockSpec(memory_space=pltpu.VMEM)
    rows = NZ * PLANE // 2 * SLOTS
    buffer = pltpu.VMEM((rows, 2 * QUARTER), BF16)
    copies = 96
    return pl.pallas_call(
        fused_kernel,
        out_shape=(
            buffer,
            buffer,
            jax.ShapeDtypeStruct((TOPK, ROWS), F32),
            jax.ShapeDtypeStruct((NZ, ROWS), jnp.int32),
        ),
        in_specs=[pl.BlockSpec(memory_space=pltpu.SMEM)] + [vmem] * 12,
        out_specs=(
            vmem,
            vmem,
            vmem,
            vmem,
        ),
        scratch_shapes=[
            pltpu.VMEM((4, V, 128), F32),
            pltpu.VMEM((V, PATCHES), BF16),
            pltpu.VMEM((V, PATCHES), BF16),
            pltpu.VMEM((HEADS, 128, PATCHES), BF16),
            pltpu.VMEM((HEADS, PATCHES, 128), BF16),
            pltpu.VMEM((HEADS, HEAD, PATCHES), BF16),
            pltpu.VMEM((BAND, 256), F32),
            pltpu.VMEM((V, 256), F32),
            pltpu.VMEM((V, 256), F32),
            pltpu.VMEM((V, 256), BF16),
            pltpu.VMEM((V, 128), BF16),
            pltpu.VMEM((V, 128), BF16),
            pltpu.VMEM((4, HALF_V, 256), BF16),
            pltpu.VMEM((4, NZ, NX, OWN_COLUMNS, HALF_V), BF16),
            pltpu.VMEM((2, 256, 256), F32),
            pltpu.VMEM((2, 256, 256), F32),
            pltpu.VMEM((16, OWN_COLUMNS, 256), BF16),
            pltpu.VMEM((8, NY, OWN_COLUMNS, ROWS), BF16),
            pltpu.VMEM((ROWS, QUARTER), BF16),
            pltpu.VMEM((TOPK, ROWS), jnp.int32),
            pltpu.VMEM((NZ, 2 * TOPK + 8, ROWS), jnp.int32),
            pltpu.VMEM((NZ, ROWS), jnp.int32),
            pltpu.VMEM((PLANE, NZ, ROWS), jnp.int32),
            pltpu.VMEM((2, NZ, ROWS, QUARTER), BF16),
            pltpu.VMEM((2, NZ, PLANE * SLOTS, QUARTER), BF16),
            pltpu.VMEM((2, 4, ROWS, 256), F32),
            pltpu.VMEM((2, TOPK, ROWS), F32),
            pltpu.SemaphoreType.DMA((copies,)),
            pltpu.SemaphoreType.DMA((copies,)),
            pltpu.SemaphoreType.DMA,
            pltpu.SemaphoreType.DMA,
            pltpu.SemaphoreType.DMA((2,)),
            pltpu.SemaphoreType.DMA((2,)),
            pltpu.SemaphoreType.DMA,
            pltpu.SemaphoreType.DMA,
        ],
        compiler_params=pltpu.CompilerParams(
            collective_id=0, has_side_effects=True, vmem_limit_bytes=46 * 1024 * 1024
        ),
    )(image_count, patches, text, ids, *norms, proj, pout, merger, tgain, router)


def interleave_kernel(counts_ref, text_ref, image_ref, out_ref, sem):
    def pair_rows(ref, k):
        return ref.at[pl.ds(pl.multiple_of(k * SLOTS, SLOTS), SLOTS)]

    def step(k, carry):
        first = counts_ref[k // (PLANE // 2), 2 * lax.rem(k, PLANE // 2)]
        pltpu.make_async_copy(pair_rows(text_ref, k), pair_rows(out_ref, 2 * k + first), sem).start()
        pltpu.make_async_copy(
            pair_rows(image_ref, k), pair_rows(out_ref, 2 * k + 1 - first), sem
        ).start()
        return carry

    lax.fori_loop(0, NZ * PLANE // 2, step, 0)
    pltpu.make_async_copy(out_ref, out_ref, sem).wait()


def interleave(counts, text_rows, image_rows):
    return pl.pallas_call(
        interleave_kernel,
        out_shape=jax.ShapeDtypeStruct((2 * text_rows.shape[0], text_rows.shape[1]), BF16),
        in_specs=[
            pl.BlockSpec(memory_space=pltpu.SMEM),
            pl.BlockSpec(memory_space=pltpu.VMEM),
            pl.BlockSpec(memory_space=pltpu.VMEM),
        ],
        out_specs=pl.BlockSpec(memory_space=pl.ANY),
        scratch_shapes=[pltpu.SemaphoreType.DMA],
    )(counts, text_rows, image_rows)


def per_device(
    patches,
    image_count,
    text_tokens,
    norm_gain,
    norm_bias,
    patch_proj,
    patch_out,
    merge_gain,
    merge_bias,
    merger,
    token_gain,
    router,
    expert_ids,
):
    text_rows, image_rows, gates, counts = fused(
        image_count,
        patches.T,
        text_tokens,
        expert_ids.T,
        (norm_gain, norm_bias, merge_gain, merge_bias),
        patch_proj.transpose(1, 2, 0),
        patch_out,
        merger.transpose(0, 2, 1),
        token_gain,
        router.reshape(2, QUARTER, router.shape[1]),
    )
    return interleave(counts, text_rows, image_rows)[None], gates.T


def solution(mesh):
    return jax.shard_map(
        per_device,
        mesh=mesh,
        in_specs=(
            P("dep", "tp"),
            P("dep"),
            P("dep", "tp"),
            P(),
            P(),
            P(None, None, "tp"),
            P("tp", None),
            P(),
            P(),
            P(None, "tp", "dep"),
            P("tp"),
            P("tp", None),
            P("dep", None),
        ),
        out_specs=(P("dep", None, "tp"), P("dep", None)),
        check_vma=False,
    )
```

```python
import math

import jax
import jax.numpy as jnp
from jax import lax
from jax.experimental import pallas as pl
from jax.experimental.pallas import tpu as pltpu
from jax.sharding import PartitionSpec as P

MESH = pl.DeviceIdType.MESH
BF16 = jnp.bfloat16
F32 = jnp.float32
NZ = 8
NX = 4
NY = 4
PLANE = NX * NY
SLOTS = 16
ROWS = 128
TOPK = 8
D = 4096
QUARTER = 1024
V = 1152
HALF_V = 576
PATCHES = 512
HEADS = 4
HEAD = 72
BAND = 288
OWN_COLUMNS = 32
EPS = 1e-06
TEXT = 0
IMAGE = 1


def selection(ids, first_expert):
    experts = first_expert + lax.broadcasted_iota(jnp.int32, (PLANE, ROWS), 0)
    count = jnp.zeros((PLANE, ROWS), F32)
    for k in range(TOPK):
        count += (ids[k : k + 1, :] == experts).astype(F32)
    earlier = (
        lax.broadcasted_iota(jnp.int32, (ROWS, ROWS), 0)
        < lax.broadcasted_iota(jnp.int32, (ROWS, ROWS), 1)
    ).astype(BF16)
    before = jnp.dot(count.astype(BF16), earlier, preferred_element_type=F32)
    slot = lax.broadcasted_iota(jnp.int32, (PLANE, SLOTS, ROWS), 1).astype(F32)
    first = before[:, None, :]
    last = (before + count)[:, None, :]
    chosen = (slot >= first) & (slot < last)
    return jnp.where(chosen, 1.0, 0.0).astype(BF16).reshape(PLANE * SLOTS, ROWS)


def fused_kernel(
    image_ref,
    patches_hbm,
    text_hbm,
    ids_ref,
    norm_gain_ref,
    norm_bias_ref,
    merge_gain_ref,
    merge_bias_ref,
    proj_hbm,
    pout_hbm,
    merger_hbm,
    tgain_ref,
    router_hbm,
    text_out,
    image_out,
    gate_ref,
    counts_ref,
    patches_ref,
    text_ref,
    proj_ref,
    pout_ref,
    merger_ref,
    router_ref,
    cols,
    pix,
    normed,
    qs,
    ks,
    vs,
    ctx,
    part_send,
    part_recv,
    merged,
    merged_peer,
    merged_mine,
    acts,
    weights,
    vis_send,
    vis_recv,
    vis,
    vis_all,
    image_rows,
    text_peer,
    ids_peer,
    held_ids,
    plane_counts,
    all_counts,
    held,
    stage,
    square_parts,
    gate_parts,
    load_sems,
    send_sems,
    recv_sems,
    acts_recv,
    vis_all_recv,
    out_send,
    out_recv,
    counts_send,
    counts_recv,
):
    dep = lax.axis_index("dep")
    h = lax.axis_index("tp")
    z = dep // PLANE
    xy = lax.rem(dep, PLANE)
    x = xy // NY
    y = lax.rem(xy, NY)
    pair = y // 2
    p = lax.rem(y, 2)
    outs = (text_out, image_out)

    def at(to_z, to_x, to_y):
        return to_z * PLANE + to_x * NY + to_y

    def along_z(step):
        return {"dep": at(lax.rem(z + NZ + step, NZ), x, y)}

    def along_x(step):
        return {"dep": at(z, lax.rem(x + NX + step, NX), y)}

    def along_y(step):
        return at(z, x, lax.rem(y + step, NY))

    def in_plane(step):
        mixed = lax.rem(7 * step, PLANE)
        to_x = lax.rem(x + mixed // NY, NX)
        to_y = lax.rem(y + lax.rem(mixed, NY), NY)
        return to_x * NY + to_y

    loads = []
    for n, (source, target) in enumerate(
        (
            (patches_hbm, patches_ref),
            (merger_hbm, merger_ref),
            (text_hbm, text_ref),
            (proj_hbm, proj_ref),
            (router_hbm, router_ref),
            (pout_hbm, pout_ref),
        )
    ):
        load = pltpu.make_async_copy(source, target, load_sems.at[n])
        load.start()
        loads.append(load)

    barrier = pltpu.get_barrier_semaphore()

    def greet(device):
        pl.semaphore_signal(barrier, inc=1, device_id=device, device_id_type=MESH)

    for step in range(1, NZ):
        greet(along_z(step))

    def greet_plane(step, carry):
        greet({"dep": z * PLANE + in_plane(step)})
        return carry

    lax.fori_loop(1, PLANE, greet_plane, 0)
    for step in range(NY):
        greet({"dep": along_y(step), "tp": 1 - h})

    other_chip = dep + 1 - 2 * p
    number = [0]
    started = []

    def remote(source, target, device, arrival=None):
        n = number[0]
        number[0] += 1
        copy = pltpu.make_async_remote_copy(
            src_ref=source,
            dst_ref=target,
            send_sem=send_sems.at[n],
            recv_sem=recv_sems.at[n] if arrival is None else arrival,
            device_id=device,
            device_id_type=MESH,
        )
        copy.start()
        started.append(copy)
        return copy

    def flag(shape):
        return jnp.full(shape, image_ref[0], jnp.int32) == 1

    row_from = lax.broadcasted_iota(jnp.int32, (PATCHES, PATCHES), 0)
    row_to = lax.broadcasted_iota(jnp.int32, (PATCHES, PATCHES), 1)
    order = jnp.where(
        row_from == 4 * lax.rem(row_to, ROWS) + row_to // ROWS, 1.0, 0.0
    ).astype(BF16)
    mine = pl.ds(pl.multiple_of(h * HALF_V, HALF_V), HALF_V)
    loads[0].wait()
    pix[mine, :] = jnp.dot(patches_ref[...], order, preferred_element_type=F32).astype(BF16)
    loads[1].wait()
    for j in range(2):
        weights[j, z, x] = jnp.concatenate([merger_ref[2 * j], merger_ref[2 * j + 1]], 1)
    loads[2].wait()

    pl.semaphore_wait(barrier, NZ - 1 + PLANE - 1 + NY)

    text_columns = pl.ds(pl.multiple_of((1 - p) * QUARTER, QUARTER), QUARTER)
    my_columns = pl.ds(pl.multiple_of(p * QUARTER, QUARTER), QUARTER)
    pix_copy = remote(pix.at[mine], pix.at[mine], {"tp": 1 - h})
    ids_copy = remote(ids_ref, ids_peer, {"dep": other_chip})
    text_copy = remote(text_ref.at[:, text_columns], text_peer, {"dep": other_chip})
    across_x = [
        remote(weights.at[0, z, x], weights.at[0, z, x], along_x(step)) for step in (1, 3, 2)
    ]

    def both_ways(right, left, along):
        return (
            remote(right, right, along(1)),
            remote(left, left, along(-1)),
        )

    def z_hop_a(step):
        back, ahead = lax.rem(z + NZ + 1 - step, NZ), lax.rem(z + step - 1, NZ)
        right = pl.ds(0, 4 if step < 4 else 2)
        left = right if step < 4 else pl.ds(2, 2)
        return both_ways(weights.at[0, back, right], weights.at[0, ahead, left], along_z)

    def z_hop_b(step):
        back, ahead = lax.rem(z + NZ + 1 - step, NZ), lax.rem(z + step - 1, NZ)
        right = pl.ds(0, OWN_COLUMNS if step < 4 else OWN_COLUMNS // 2)
        left = right if step < 4 else pl.ds(OWN_COLUMNS // 2, OWN_COLUMNS // 2)
        return both_ways(weights.at[1, back, x, right], weights.at[1, ahead, x, left], along_z)

    def x_hop_b(step):
        back, ahead = lax.rem(x + NX + 1 - step, NX), lax.rem(x + step - 1, NX)
        right = pl.ds(0, NZ if step < 2 else NZ // 2)
        left = right if step < 2 else pl.ds(NZ // 2, NZ // 2)
        return both_ways(weights.at[1, right, back], weights.at[1, left, ahead], along_x)

    def arrived(copies):
        for copy in copies:
            copy.wait_recv()

    hop_b = z_hop_b(1)

    for v, vector in enumerate((norm_gain_ref, norm_bias_ref, merge_gain_ref, merge_bias_ref)):
        for c in range(0, V, 128):
            row = jnp.broadcast_to(vector[c : c + 128].reshape(1, 128), (128, 128))
            cols[v, c : c + 128, :] = row.T

    def layer_norm(values, gain, bias):
        mean = jnp.sum(values, 0, keepdims=True) / V
        variance = jnp.sum(values * values, 0, keepdims=True) / V - mean * mean
        return (values - mean) * lax.rsqrt(variance + EPS) * gain + bias

    def to_unit(parts, phase):
        me = p * 2 + h
        return [
            remote(
                parts.at[phase, me],
                parts.at[phase, me],
                {"dep": dep if dp == 0 else other_chip, "tp": h if dh == 0 else 1 - h},
            )
            for dp, dh in ((0, 1), (1, 0), (1, 1))
        ]

    def total_of(parts, phase):
        return parts[phase, 0] + parts[phase, 1] + parts[phase, 2] + parts[phase, 3]

    def inv_rms(phase):
        return lax.rsqrt(total_of(square_parts, phase)[0:1, :] / D + EPS)

    def start_squares(phase, squares):
        square_parts[phase, p * 2 + h] = jnp.broadcast_to(squares, (8, ROWS))
        return to_unit(square_parts, phase)

    def start_gates(phase, hidden):
        scaled = hidden * tgain_ref[my_columns].reshape(1, QUARTER)
        logits = jnp.dot(scaled.astype(BF16), router_ref[p], preferred_element_type=F32).T
        expert = lax.broadcasted_iota(jnp.int32, (128, ROWS), 0)
        ids = held_ids[0, phase * TOPK : (phase + 1) * TOPK]
        me = p * 2 + h
        for k in range(TOPK):
            gate_parts[phase, me, k : k + 1, :] = jnp.sum(
                jnp.where(ids[k : k + 1, :] == expert, logits, 0.0), 0, keepdims=True
            )
        return to_unit(gate_parts, phase)

    def normalise(phase, hidden):
        inverse = jnp.broadcast_to(inv_rms(phase), (ROWS, ROWS)).T[:, 0:1]
        held[phase, 0] = (hidden * tgain_ref[my_columns].reshape(1, QUARTER) * inverse).astype(BF16)

    def gate(phase):
        chosen = total_of(gate_parts, phase) * inv_rms(phase)
        raised = jnp.exp(chosen - jnp.max(chosen, 0, keepdims=True))
        return raised / jnp.sum(raised, 0, keepdims=True)

    def ring_hop(phase, step):
        back, ahead = lax.rem(NZ + 1 - step, NZ), step - 1
        right = pl.ds(0, QUARTER if step < 4 else QUARTER // 2)
        left = right if step < 4 else pl.ds(QUARTER // 2, QUARTER // 2)
        return (
            remote(
                held.at[phase, back, :, right], held.at[phase, NZ - step, :, right], along_z(1)
            ),
            remote(
                held.at[phase, ahead, :, left], held.at[phase, step, :, left], along_z(NZ - 1)
            ),
        )

    def spread(phase, slot):
        ids = held_ids[slot, phase * TOPK : (phase + 1) * TOPK]
        chosen = selection(ids, z * PLANE)
        for c in range(0, QUARTER, 512):
            stage[phase, slot, :, c : c + 512] = jnp.dot(
                chosen, held[phase, slot, :, c : c + 512], preferred_element_type=F32
            ).astype(BF16)
        source_pair = lax.rem(z + slot, NZ) * (PLANE // 2) + xy // 2
        at_dest = outs[phase].at[pl.ds(source_pair * SLOTS, SLOTS), my_columns]
        pltpu.make_async_copy(
            stage.at[phase, slot, pl.ds(xy * SLOTS, SLOTS)], at_dest, out_recv.at[phase]
        ).start()

        def send(step, carry):
            peer = in_plane(step)
            pltpu.make_async_remote_copy(
                src_ref=stage.at[phase, slot, pl.ds(peer * SLOTS, SLOTS)],
                dst_ref=at_dest,
                send_sem=out_send.at[phase],
                recv_sem=out_recv.at[phase],
                device_id={"dep": z * PLANE + peer},
                device_id_type=MESH,
            ).start()
            return carry

        lax.fori_loop(1, PLANE, send, 0)

    def text_hidden():
        return jnp.where(
            flag((ROWS, QUARTER)),
            text_peer[...].astype(F32),
            text_ref[:, my_columns].astype(F32),
        )

    def text_spread(*slots):
        for slot in slots:
            if slot:
                id_copies[NZ - 1 - slot].wait_recv()
            spread(TEXT, slot)

    def attend(lanes):
        for head in range(HEADS):
            scores = jnp.dot(ks[head], qs[head, :, lanes], preferred_element_type=F32)
            below = scores - jnp.max(scores, 0, keepdims=True)
            raised = jnp.exp2(below * (math.log2(math.e) / math.sqrt(HEAD))).astype(BF16)
            product = jnp.dot(vs[head], raised, preferred_element_type=F32)
            ctx[head * HEAD : (head + 1) * HEAD, :] = product[:HEAD] / product[HEAD : HEAD + 1]
        return ctx[...].astype(BF16)

    def out_product(context, lo):
        return lax.dot_general(
            pout_ref[:, lo : lo + 384],
            context,
            (((0,), (0,)), ((), ())),
            preferred_element_type=F32,
        )

    pix_copy.wait_recv()
    for c in range(0, PATCHES, 128):
        normed[:, c : c + 128] = layer_norm(
            pix[:, c : c + 128].astype(F32), cols[0], cols[1]
        ).astype(BF16)
    loads[3].wait()
    pad = jnp.zeros((128 - HEAD, PATCHES), F32)
    queries = jnp.dot(proj_ref[0], normed[...], preferred_element_type=F32)
    for head in range(HEADS):
        part = jnp.concatenate([queries[head * HEAD : (head + 1) * HEAD], pad], 0)
        qs[head] = part.astype(BF16)
    keys = jnp.dot(proj_ref[1], normed[...], preferred_element_type=F32)
    for head in range(HEADS):
        part = jnp.concatenate([keys[head * HEAD : (head + 1) * HEAD], pad], 0)
        ks[head] = part.T.astype(BF16)
    values = jnp.dot(proj_ref[2], normed[...], preferred_element_type=F32)
    ones = jnp.ones((8, PATCHES), F32)
    for head in range(HEADS):
        part = jnp.concatenate([values[head * HEAD : (head + 1) * HEAD], ones], 0)
        vs[head] = part.astype(BF16)

    ids_copy.wait_recv()
    has = flag((TOPK, ROWS))
    held_ids[0, 0:TOPK] = jnp.where(has, ids_peer[...], ids_ref[...])
    held_ids[0, TOPK : 2 * TOPK] = jnp.where(has, ids_ref[...], ids_peer[...])
    held_ids[0, 2 * TOPK :] = jnp.full((8, ROWS), image_ref[0], jnp.int32)
    id_copies = [
        remote(held_ids.at[0], held_ids.at[NZ - step], along_z(step)) for step in range(1, NZ)
    ]

    my_rows = pl.ds(pl.multiple_of(h * 256, 256), 256)
    their_rows = pl.ds(pl.multiple_of((1 - h) * 256, 256), 256)
    context = attend(their_rows)
    loads[5].wait()
    part_copies = []
    for lo in range(0, V, 384):
        part_send[lo : lo + 384, :] = out_product(context, lo)
        block = pl.ds(lo, 384)
        part_copies.append(remote(part_send.at[block], part_recv.at[block], {"tp": 1 - h}))
    arrived(hop_b)
    hop_b = z_hop_b(2)
    arrived(across_x)
    hop_a = z_hop_a(1)
    context = attend(my_rows)
    text_copy.wait_recv()
    hidden = text_hidden()
    squares = jnp.broadcast_to(jnp.sum(hidden * hidden, 1, keepdims=True), (ROWS, ROWS))
    text_squares = start_squares(TEXT, squares.T[0:1, :])
    arrived(part_copies)
    for lo in range(0, V, 384):
        block = pl.ds(lo, 384)
        part_recv[block, :] += out_product(context, lo) + pix[block, my_rows].astype(F32)
    for c in range(0, 256, 128):
        merged[:, c : c + 128] = layer_norm(part_recv[:, c : c + 128], cols[2], cols[3]).astype(
            BF16
        )
    keep = pl.ds(pl.multiple_of(p * 128, 128), 128)
    give = pl.ds(pl.multiple_of((1 - p) * 128, 128), 128)
    merged_copy = remote(merged.at[:, give], merged_peer, {"dep": other_chip})

    arrived(text_squares)
    normalise(TEXT, text_hidden())
    ring = ring_hop(TEXT, 1)
    text_spread(0)
    arrived(hop_b)
    hop_b = z_hop_b(3)
    arrived(hop_a)
    hop_a = z_hop_a(2)
    merged_copy.wait_recv()
    merged_mine[...] = jnp.where(
        flag((V, 128)), merged[:, keep].astype(F32), merged_peer[...].astype(F32)
    ).astype(BF16)
    lanes = pl.ds(pl.multiple_of(pair * 128, 128), 128)
    own_half = merged_mine.at[mine]
    theirs = merged_mine.at[pl.ds(pl.multiple_of((1 - h) * HALF_V, HALF_V), HALF_V)]
    place = acts.at[h, pl.ds(pl.multiple_of(p * HALF_V, HALF_V), HALF_V), lanes]
    pltpu.make_async_copy(own_half, place, acts_recv).start()
    for step in (1, 3, 2, 0):
        if step > 0:
            remote(own_half, place, {"dep": along_y(step)}, acts_recv)
        remote(theirs, place, {"dep": along_y(step), "tp": 1 - h}, acts_recv)
    arrived(hop_b)
    hop_b = z_hop_b(4)
    arrived(ring)
    ring = ring_hop(TEXT, 2)
    text_spread(1, 7)
    arrived(hop_b)
    hop_b = x_hop_b(1)
    arrived(hop_a)
    hop_a = z_hop_a(3)
    arrived(ring)
    ring = ring_hop(TEXT, 3)
    text_spread(2, 6)
    arrived(hop_a)
    hop_a = z_hop_a(4)
    arrived(hop_b)
    hop_b = x_hop_b(2)
    arrived(ring)
    ring = ring_hop(TEXT, 4)
    text_spread(3, 5)
    arrived(ring)
    text_spread(4)
    loads[4].wait()
    text_gates = start_gates(TEXT, text_hidden())
    for slot in range(NZ):
        plane_counts[pl.ds(lax.rem(z + slot, NZ), 1), :] = held_ids[slot, 2 * TOPK : 2 * TOPK + 1]
    all_counts[xy] = plane_counts[...]

    def send_counts(step, carry):
        pltpu.make_async_remote_copy(
            src_ref=plane_counts,
            dst_ref=all_counts.at[xy],
            send_sem=counts_send,
            recv_sem=counts_recv,
            device_id={"dep": z * PLANE + in_plane(step)},
            device_id_type=MESH,
        ).start()
        return carry

    lax.fori_loop(1, PLANE, send_counts, 0)
    arrived(hop_a)
    arrived(hop_b)
    pltpu.make_async_copy(acts, acts, acts_recv).wait()

    def columns_of(zs):
        total = None
        for j in range(2):
            block = weights[j, pl.ds(zs, 2)].reshape(2 * NX * OWN_COLUMNS, V)
            product = jnp.dot(block, acts[j], preferred_element_type=F32)
            total = product if total is None else total + product
        return total

    vis_copies = []
    for c in range(2):
        vis_send[c] = columns_of((1 - h) * 4 + 2 * c)
        vis_copies.append(remote(vis_send.at[c], vis_recv.at[c], {"tp": 1 - h}))
    for c in range(2):
        product = columns_of(h * 4 + 2 * c)
        vis_copies[c].wait_recv()
        vis[pl.ds(8 * c, 8)] = (product + vis_recv[c]).astype(BF16).reshape(8, OWN_COLUMNS, 256)

    def vis_block(to_y):
        return vis.at[
            pl.ds(lax.rem(to_y, 2) * 8, 8), :, pl.ds(pl.multiple_of((to_y // 2) * 128, 128), 128)
        ]

    pltpu.make_async_copy(vis_block(y), vis_all.at[:, y], vis_all_recv).start()
    for step in range(1, NY):
        to_y = lax.rem(y + step, NY)
        remote(vis_block(to_y), vis_all.at[:, y], {"dep": along_y(step)}, vis_all_recv)
    pltpu.make_async_copy(vis_all, vis_all, vis_all_recv).wait()

    hidden = vis_all[...].reshape(QUARTER, ROWS).astype(F32)
    image_squares = start_squares(IMAGE, jnp.sum(hidden * hidden, 0, keepdims=True))
    image_rows[...] = hidden.T
    arrived(image_squares)
    normalise(IMAGE, image_rows[...])
    ring = ring_hop(IMAGE, 1)
    spread(IMAGE, 0)
    image_gates = start_gates(IMAGE, image_rows[...])
    for step in range(1, 5):
        arrived(ring)
        if step < 4:
            ring = ring_hop(IMAGE, step + 1)
        for slot in (step, NZ - step) if step < 4 else (4,):
            spread(IMAGE, slot)
    arrived(text_gates)
    arrived(image_gates)
    gate_ref[...] = jnp.where(flag((TOPK, ROWS)), gate(IMAGE), gate(TEXT))

    for copy in started:
        copy.wait_send()
    others = all_counts.at[pl.ds(0, PLANE - 1)]
    pltpu.make_async_copy(others, others, counts_send).wait()
    pltpu.make_async_copy(others, others, counts_recv).wait()
    lane = lax.broadcasted_iota(jnp.int32, (NZ, ROWS), 1)
    total_counts = jnp.zeros((NZ, ROWS), jnp.int32)
    for source in range(PLANE):
        total_counts += jnp.where(lane == source, all_counts[source], 0)
    counts_ref[...] = total_counts
    for phase in (TEXT, IMAGE):
        sent = stage.at[phase, :, pl.ds(0, (PLANE - 1) * SLOTS)]
        pltpu.make_async_copy(sent, sent, out_send.at[phase]).wait()
        pltpu.make_async_copy(outs[phase], outs[phase], out_recv.at[phase]).wait()


def fused(image_count, patches, text, ids, norms, proj, pout, merger, tgain, router):
    vmem = pl.BlockSpec(memory_space=pltpu.VMEM)
    hbm = pl.BlockSpec(memory_space=pl.ANY)
    loaded = (patches, text, proj, pout, merger, router)
    rows = NZ * PLANE // 2 * SLOTS
    buffer = pltpu.VMEM((rows, 2 * QUARTER), BF16)
    copies = 96
    return pl.pallas_call(
        fused_kernel,
        out_shape=(
            buffer,
            buffer,
            pltpu.VMEM((TOPK, ROWS), F32),
            pltpu.VMEM((NZ, ROWS), jnp.int32),
        ),
        in_specs=[pl.BlockSpec(memory_space=pltpu.SMEM), hbm, hbm]
        + [vmem] * 5
        + [hbm] * 3
        + [vmem, hbm],
        out_specs=(
            vmem,
            vmem,
            vmem,
            vmem,
        ),
        scratch_shapes=[pltpu.VMEM(a.shape, a.dtype) for a in loaded]
        + [
            pltpu.VMEM((4, V, 128), F32),
            pltpu.VMEM((V, PATCHES), BF16),
            pltpu.VMEM((V, PATCHES), BF16),
            pltpu.VMEM((HEADS, 128, PATCHES), BF16),
            pltpu.VMEM((HEADS, PATCHES, 128), BF16),
            pltpu.VMEM((HEADS, HEAD + 8, PATCHES), BF16),
            pltpu.VMEM((BAND, 256), F32),
            pltpu.VMEM((V, 256), F32),
            pltpu.VMEM((V, 256), F32),
            pltpu.VMEM((V, 256), BF16),
            pltpu.VMEM((V, 128), BF16),
            pltpu.VMEM((V, 128), BF16),
            pltpu.VMEM((2, V, 256), BF16),
            pltpu.VMEM((2, NZ, NX, OWN_COLUMNS, V), BF16),
            pltpu.VMEM((2, 256, 256), F32),
            pltpu.VMEM((2, 256, 256), F32),
            pltpu.VMEM((16, OWN_COLUMNS, 256), BF16),
            pltpu.VMEM((8, NY, OWN_COLUMNS, ROWS), BF16),
            pltpu.VMEM((ROWS, QUARTER), F32),
            pltpu.VMEM((ROWS, QUARTER), BF16),
            pltpu.VMEM((TOPK, ROWS), jnp.int32),
            pltpu.VMEM((NZ, 2 * TOPK + 8, ROWS), jnp.int32),
            pltpu.VMEM((NZ, ROWS), jnp.int32),
            pltpu.VMEM((PLANE, NZ, ROWS), jnp.int32),
            pltpu.VMEM((2, NZ, ROWS, QUARTER), BF16),
            pltpu.VMEM((2, NZ, PLANE * SLOTS, QUARTER), BF16),
            pltpu.VMEM((2, 4, 8, ROWS), F32),
            pltpu.VMEM((2, 4, TOPK, ROWS), F32),
            pltpu.SemaphoreType.DMA((6,)),
            pltpu.SemaphoreType.DMA((copies,)),
            pltpu.SemaphoreType.DMA((copies,)),
            pltpu.SemaphoreType.DMA,
            pltpu.SemaphoreType.DMA,
            pltpu.SemaphoreType.DMA((2,)),
            pltpu.SemaphoreType.DMA((2,)),
            pltpu.SemaphoreType.DMA,
            pltpu.SemaphoreType.DMA,
        ],
        compiler_params=pltpu.CompilerParams(
            collective_id=0, has_side_effects=True, vmem_limit_bytes=46 * 1024 * 1024
        ),
    )(image_count, patches, text, ids, *norms, proj, pout, merger, tgain, router)


def interleave_kernel(counts_ref, text_ref, image_ref, gate_ref, out_ref, gate_out, sem):
    def pair_rows(ref, k):
        return ref.at[pl.ds(pl.multiple_of(k * SLOTS, SLOTS), SLOTS)]

    def step(k, carry):
        first = counts_ref[k // (PLANE // 2), 2 * lax.rem(k, PLANE // 2)]
        pltpu.make_async_copy(pair_rows(text_ref, k), pair_rows(out_ref, 2 * k + first), sem).start(
            priority=0
        )
        pltpu.make_async_copy(
            pair_rows(image_ref, k), pair_rows(out_ref, 2 * k + 1 - first), sem
        ).start(priority=1)
        return carry

    lax.fori_loop(0, NZ * PLANE // 2, step, 0)
    gate_out[...] = gate_ref[...]
    pltpu.make_async_copy(out_ref, out_ref, sem).wait()


def interleave(counts, text_rows, image_rows, gates):
    vmem = pl.BlockSpec(memory_space=pltpu.VMEM)
    held = pl.BlockSpec(memory_space=pl.ANY)
    return pl.pallas_call(
        interleave_kernel,
        out_shape=(
            jax.ShapeDtypeStruct((2 * text_rows.shape[0], text_rows.shape[1]), BF16),
            jax.ShapeDtypeStruct(gates.shape, F32),
        ),
        in_specs=[pl.BlockSpec(memory_space=pltpu.SMEM), held, held, vmem],
        out_specs=(held, vmem),
        scratch_shapes=[pltpu.SemaphoreType.DMA],
        compiler_params=pltpu.CompilerParams(vmem_limit_bytes=4 * 1024 * 1024),
    )(counts, text_rows, image_rows, gates)


def per_device(
    patches,
    image_count,
    text_tokens,
    norm_gain,
    norm_bias,
    patch_proj,
    patch_out,
    merge_gain,
    merge_bias,
    merger,
    token_gain,
    router,
    expert_ids,
):
    text_rows, image_rows, gates, counts = fused(
        image_count,
        patches.T,
        text_tokens,
        expert_ids.T,
        (norm_gain, norm_bias, merge_gain, merge_bias),
        patch_proj.transpose(1, 2, 0),
        patch_out,
        merger.transpose(0, 2, 1),
        token_gain,
        router.reshape(2, QUARTER, router.shape[1]),
    )
    dispatched, gate_probs = interleave(counts, text_rows, image_rows, gates)
    return dispatched[None], gate_probs.T


def solution(mesh):
    return jax.shard_map(
        per_device,
        mesh=mesh,
        in_specs=(
            P("dep", "tp"),
            P("dep"),
            P("dep", "tp"),
            P(),
            P(),
            P(None, None, "tp"),
            P("tp", None),
            P(),
            P(),
            P(None, "tp", "dep"),
            P("tp"),
            P("tp", None),
            P("dep", None),
        ),
        out_specs=(P("dep", None, "tp"), P("dep", None)),
        check_vma=False,
    )
```

```python
import math

import jax
import jax.numpy as jnp
from jax import lax
from jax.experimental import pallas as pl
from jax.experimental.pallas import tpu as pltpu
from jax.sharding import PartitionSpec as P

MESH = pl.DeviceIdType.MESH
BF16 = jnp.bfloat16
F32 = jnp.float32
NZ = 8
NX = 4
NY = 4
PLANE = NX * NY
SLOTS = 16
ROWS = 128
TOPK = 8
D = 4096
QUARTER = 1024
V = 1152
HALF_V = 576
PATCHES = 512
HEADS = 4
HEAD = 72
BAND = 288
OWN_COLUMNS = 32
EPS = 1e-06
TEXT = 0
IMAGE = 1


def selection(ids, first_expert):
    experts = first_expert + lax.broadcasted_iota(jnp.int32, (PLANE, ROWS), 0)
    count = jnp.zeros((PLANE, ROWS), F32)
    for k in range(TOPK):
        count += (ids[k : k + 1, :] == experts).astype(F32)
    earlier = (
        lax.broadcasted_iota(jnp.int32, (ROWS, ROWS), 0)
        < lax.broadcasted_iota(jnp.int32, (ROWS, ROWS), 1)
    ).astype(BF16)
    before = jnp.dot(count.astype(BF16), earlier, preferred_element_type=F32)
    slot = lax.broadcasted_iota(jnp.int32, (PLANE, SLOTS, ROWS), 1).astype(F32)
    first = before[:, None, :]
    last = (before + count)[:, None, :]
    chosen = (slot >= first) & (slot < last)
    return jnp.where(chosen, 1.0, 0.0).astype(BF16).reshape(PLANE * SLOTS, ROWS)


def fused_kernel(
    image_ref,
    patches_hbm,
    text_hbm,
    ids_ref,
    norm_gain_ref,
    norm_bias_ref,
    merge_gain_ref,
    merge_bias_ref,
    proj_hbm,
    pout_hbm,
    merger_hbm,
    tgain_ref,
    router_hbm,
    text_out,
    image_out,
    gate_ref,
    counts_ref,
    patches_ref,
    text_ref,
    proj_ref,
    pout_ref,
    merger_ref,
    router_ref,
    cols,
    pix,
    normed,
    qs,
    ks,
    vs,
    ctx,
    part_send,
    part_recv,
    merged,
    merged_peer,
    merged_mine,
    acts,
    weights,
    vis_send,
    vis_recv,
    vis,
    vis_all,
    image_rows,
    text_peer,
    text_normed,
    text_squares,
    text_chosen,
    ids_peer,
    held_ids,
    plane_counts,
    all_counts,
    held,
    stage,
    square_parts,
    gate_parts,
    load_sems,
    send_sems,
    recv_sems,
    acts_recv,
    vis_all_recv,
    out_send,
    out_recv,
    counts_send,
    counts_recv,
):
    dep = lax.axis_index("dep")
    h = lax.axis_index("tp")
    z = dep // PLANE
    xy = lax.rem(dep, PLANE)
    x = xy // NY
    y = lax.rem(xy, NY)
    pair = y // 2
    p = lax.rem(y, 2)
    outs = (text_out, image_out)

    def at(to_z, to_x, to_y):
        return to_z * PLANE + to_x * NY + to_y

    def along_z(step):
        return {"dep": at(lax.rem(z + NZ + step, NZ), x, y)}

    def along_x(step):
        return {"dep": at(z, lax.rem(x + NX + step, NX), y)}

    def along_y(step):
        return at(z, x, lax.rem(y + step, NY))

    def in_plane(step):
        mixed = lax.rem(7 * step, PLANE)
        to_x = lax.rem(x + mixed // NY, NX)
        to_y = lax.rem(y + lax.rem(mixed, NY), NY)
        return to_x * NY + to_y

    loads = []
    for n, (source, target) in enumerate(
        (
            (patches_hbm, patches_ref),
            (merger_hbm, merger_ref),
            (text_hbm, text_ref),
            (proj_hbm, proj_ref),
            (router_hbm, router_ref),
            (pout_hbm, pout_ref),
        )
    ):
        load = pltpu.make_async_copy(source, target, load_sems.at[n])
        load.start()
        loads.append(load)

    barrier = pltpu.get_barrier_semaphore()

    def greet(device):
        pl.semaphore_signal(barrier, inc=1, device_id=device, device_id_type=MESH)

    for step in range(1, NZ):
        greet(along_z(step))

    def greet_plane(step, carry):
        greet({"dep": z * PLANE + in_plane(step)})
        return carry

    lax.fori_loop(1, PLANE, greet_plane, 0)
    for step in range(NY):
        greet({"dep": along_y(step), "tp": 1 - h})

    other_chip = dep + 1 - 2 * p
    number = [0]
    started = []

    def remote(source, target, device, arrival=None):
        n = number[0]
        number[0] += 1
        copy = pltpu.make_async_remote_copy(
            src_ref=source,
            dst_ref=target,
            send_sem=send_sems.at[n],
            recv_sem=recv_sems.at[n] if arrival is None else arrival,
            device_id=device,
            device_id_type=MESH,
        )
        copy.start()
        started.append(copy)
        return copy

    def flag(shape):
        return jnp.full(shape, image_ref[0], jnp.int32) == 1

    row_from = lax.broadcasted_iota(jnp.int32, (PATCHES, PATCHES), 0)
    row_to = lax.broadcasted_iota(jnp.int32, (PATCHES, PATCHES), 1)
    order = jnp.where(
        row_from == 4 * lax.rem(row_to, ROWS) + row_to // ROWS, 1.0, 0.0
    ).astype(BF16)
    mine = pl.ds(pl.multiple_of(h * HALF_V, HALF_V), HALF_V)
    loads[0].wait()
    pix[mine, :] = jnp.dot(patches_ref[...], order, preferred_element_type=F32).astype(BF16)
    loads[1].wait()
    for j in range(2):
        weights[j, z, x] = jnp.concatenate([merger_ref[2 * j], merger_ref[2 * j + 1]], 1)
    loads[2].wait()
    raw = text_ref[...].astype(F32)
    squares = jnp.broadcast_to(jnp.sum(raw * raw, 1, keepdims=True), (ROWS, ROWS))
    text_squares[h] = jnp.broadcast_to(squares.T[0:1, :], (8, ROWS))

    pl.semaphore_wait(barrier, NZ - 1 + PLANE - 1 + NY)

    text_columns = pl.ds(pl.multiple_of((1 - p) * QUARTER, QUARTER), QUARTER)
    my_columns = pl.ds(pl.multiple_of(p * QUARTER, QUARTER), QUARTER)
    squares_copy = remote(text_squares.at[h], text_squares.at[h], {"tp": 1 - h})
    pix_copy = remote(pix.at[mine], pix.at[mine], {"tp": 1 - h})
    ids_copy = remote(ids_ref, ids_peer, {"dep": other_chip})
    across_x = [
        remote(weights.at[0, z, x], weights.at[0, z, x], along_x(step)) for step in (1, 3, 2)
    ]

    def both_ways(right, left, along):
        return (
            remote(right, right, along(1)),
            remote(left, left, along(-1)),
        )

    def z_hop_a(step):
        back, ahead = lax.rem(z + NZ + 1 - step, NZ), lax.rem(z + step - 1, NZ)
        right = pl.ds(0, 4 if step < 4 else 2)
        left = right if step < 4 else pl.ds(2, 2)
        return both_ways(weights.at[0, back, right], weights.at[0, ahead, left], along_z)

    def z_hop_b(step):
        back, ahead = lax.rem(z + NZ + 1 - step, NZ), lax.rem(z + step - 1, NZ)
        right = pl.ds(0, OWN_COLUMNS if step < 4 else OWN_COLUMNS // 2)
        left = right if step < 4 else pl.ds(OWN_COLUMNS // 2, OWN_COLUMNS // 2)
        return both_ways(weights.at[1, back, x, right], weights.at[1, ahead, x, left], along_z)

    def arrived(copies):
        for copy in copies:
            copy.wait_recv()

    def x_send_b(*blocks):
        for block in blocks:
            to_share = weights.at[1, lax.rem(z + NZ + block, NZ), x]
            for step in (1, 3, 2):
                shared.append(remote(to_share, to_share, along_x(step)))

    shared = []
    hop_b = z_hop_b(1)
    x_send_b(0)

    squares_copy.wait_recv()
    text_inverse = lax.rsqrt((text_squares[0] + text_squares[1]) / D + EPS)[0:1, :]
    inverse = jnp.broadcast_to(text_inverse, (ROWS, ROWS)).T[:, 0:1]
    text_normed[...] = (
        text_ref[...].astype(F32) * tgain_ref[...].reshape(1, 2 * QUARTER) * inverse
    ).astype(BF16)
    text_copy = remote(text_normed.at[:, text_columns], text_peer, {"dep": other_chip})

    for v, vector in enumerate((norm_gain_ref, norm_bias_ref, merge_gain_ref, merge_bias_ref)):
        for c in range(0, V, 128):
            row = jnp.broadcast_to(vector[c : c + 128].reshape(1, 128), (128, 128))
            cols[v, c : c + 128, :] = row.T

    def layer_norm(values, gain, bias):
        mean = jnp.sum(values, 0, keepdims=True) / V
        variance = jnp.sum(values * values, 0, keepdims=True) / V - mean * mean
        return (values - mean) * lax.rsqrt(variance + EPS) * gain + bias

    def to_unit(parts):
        me = p * 2 + h
        return [
            remote(
                parts.at[me],
                parts.at[me],
                {"dep": dep if dp == 0 else other_chip, "tp": h if dh == 0 else 1 - h},
            )
            for dp, dh in ((0, 1), (1, 0), (1, 1))
        ]

    def total_of(parts):
        return parts[0] + parts[1] + parts[2] + parts[3]

    def chosen_logits(scaled, weight, ids):
        logits = jnp.dot(scaled.astype(BF16), weight, preferred_element_type=F32).T
        expert = lax.broadcasted_iota(jnp.int32, (128, ROWS), 0)
        return jnp.concatenate(
            [
                jnp.sum(jnp.where(ids[k : k + 1, :] == expert, logits, 0.0), 0, keepdims=True)
                for k in range(TOPK)
            ],
            0,
        )

    def gate(chosen):
        raised = jnp.exp(chosen - jnp.max(chosen, 0, keepdims=True))
        return raised / jnp.sum(raised, 0, keepdims=True)

    def ring_hop(phase, step):
        back, ahead = lax.rem(NZ + 1 - step, NZ), step - 1
        right = pl.ds(0, QUARTER if step < 4 else QUARTER // 2)
        left = right if step < 4 else pl.ds(QUARTER // 2, QUARTER // 2)
        return (
            remote(
                held.at[phase, back, :, right], held.at[phase, NZ - step, :, right], along_z(1)
            ),
            remote(
                held.at[phase, ahead, :, left], held.at[phase, step, :, left], along_z(NZ - 1)
            ),
        )

    def spread(phase, slot):
        ids = held_ids[slot, phase * TOPK : (phase + 1) * TOPK]
        chosen = selection(ids, z * PLANE)
        for c in range(0, QUARTER, 512):
            stage[phase, slot, :, c : c + 512] = jnp.dot(
                chosen, held[phase, slot, :, c : c + 512], preferred_element_type=F32
            ).astype(BF16)
        source_pair = lax.rem(z + slot, NZ) * (PLANE // 2) + xy // 2
        at_dest = outs[phase].at[pl.ds(source_pair * SLOTS, SLOTS), my_columns]
        pltpu.make_async_copy(
            stage.at[phase, slot, pl.ds(xy * SLOTS, SLOTS)], at_dest, out_recv.at[phase]
        ).start()

        def send(step, carry):
            peer = in_plane(step)
            pltpu.make_async_remote_copy(
                src_ref=stage.at[phase, slot, pl.ds(peer * SLOTS, SLOTS)],
                dst_ref=at_dest,
                send_sem=out_send.at[phase],
                recv_sem=out_recv.at[phase],
                device_id={"dep": z * PLANE + peer},
                device_id_type=MESH,
            ).start()
            return carry

        lax.fori_loop(1, PLANE, send, 0)

    def text_spread(*slots):
        for slot in slots:
            spread(TEXT, slot)

    def attend(lanes):
        for head in range(HEADS):
            scores = jnp.dot(ks[head], qs[head, :, lanes], preferred_element_type=F32)
            below = scores - jnp.max(scores, 0, keepdims=True)
            raised = jnp.exp2(below * (math.log2(math.e) / math.sqrt(HEAD))).astype(BF16)
            product = jnp.dot(vs[head], raised, preferred_element_type=F32)
            ctx[head * HEAD : (head + 1) * HEAD, :] = product[:HEAD] / product[HEAD : HEAD + 1]
        return ctx[...].astype(BF16)

    def out_product(context, lo):
        return lax.dot_general(
            pout_ref[:, lo : lo + 384],
            context,
            (((0,), (0,)), ((), ())),
            preferred_element_type=F32,
        )

    pix_copy.wait_recv()
    for c in range(0, PATCHES, 128):
        normed[:, c : c + 128] = layer_norm(
            pix[:, c : c + 128].astype(F32), cols[0], cols[1]
        ).astype(BF16)
    loads[3].wait()
    pad = jnp.zeros((128 - HEAD, PATCHES), F32)
    queries = jnp.dot(proj_ref[0], normed[...], preferred_element_type=F32)
    for head in range(HEADS):
        part = jnp.concatenate([queries[head * HEAD : (head + 1) * HEAD], pad], 0)
        qs[head] = part.astype(BF16)
    keys = jnp.dot(proj_ref[1], normed[...], preferred_element_type=F32)
    for head in range(HEADS):
        part = jnp.concatenate([keys[head * HEAD : (head + 1) * HEAD], pad], 0)
        ks[head] = part.T.astype(BF16)
    values = jnp.dot(proj_ref[2], normed[...], preferred_element_type=F32)
    ones = jnp.ones((8, PATCHES), F32)
    for head in range(HEADS):
        part = jnp.concatenate([values[head * HEAD : (head + 1) * HEAD], ones], 0)
        vs[head] = part.astype(BF16)

    ids_copy.wait_recv()
    has = flag((TOPK, ROWS))
    held_ids[0, 0:TOPK] = jnp.where(has, ids_peer[...], ids_ref[...])
    held_ids[0, TOPK : 2 * TOPK] = jnp.where(has, ids_ref[...], ids_peer[...])
    held_ids[0, 2 * TOPK :] = jnp.full((8, ROWS), image_ref[0], jnp.int32)
    id_copies = [
        remote(held_ids.at[0], held_ids.at[NZ - step], along_z(step)) for step in range(1, NZ)
    ]

    my_rows = pl.ds(pl.multiple_of(h * 256, 256), 256)
    their_rows = pl.ds(pl.multiple_of((1 - h) * 256, 256), 256)
    context = attend(their_rows)
    loads[5].wait()
    part_copies = []
    for lo in range(0, V, 384):
        part_send[lo : lo + 384, :] = out_product(context, lo)
        block = pl.ds(lo, 384)
        part_copies.append(remote(part_send.at[block], part_recv.at[block], {"tp": 1 - h}))
    arrived(hop_b)
    hop_b = z_hop_b(2)
    x_send_b(1, -1)
    arrived(across_x)
    hop_a = z_hop_a(1)
    text_copy.wait_recv()
    held[TEXT, 0] = jnp.where(
        flag((ROWS, QUARTER)), text_peer[...].astype(F32), text_normed[:, my_columns].astype(F32)
    ).astype(BF16)
    ring = ring_hop(TEXT, 1)
    text_spread(0)
    context = attend(my_rows)
    arrived(hop_b)
    hop_b = z_hop_b(3)
    x_send_b(2, -2)
    arrived(part_copies)
    for lo in range(0, V, 384):
        block = pl.ds(lo, 384)
        part_recv[block, :] += out_product(context, lo) + pix[block, my_rows].astype(F32)
    for c in range(0, 256, 128):
        merged[:, c : c + 128] = layer_norm(part_recv[:, c : c + 128], cols[2], cols[3]).astype(
            BF16
        )
    keep = pl.ds(pl.multiple_of(p * 128, 128), 128)
    give = pl.ds(pl.multiple_of((1 - p) * 128, 128), 128)
    merged_copy = remote(merged.at[:, give], merged_peer, {"dep": other_chip})

    arrived(hop_b)
    hop_b = z_hop_b(4)
    x_send_b(3, -3)
    arrived(hop_a)
    hop_a = z_hop_a(2)
    arrived(ring)
    ring = ring_hop(TEXT, 2)
    arrived(id_copies)
    text_spread(1, 7)
    arrived(hop_b)
    x_send_b(4)
    merged_copy.wait_recv()
    merged_mine[...] = jnp.where(
        flag((V, 128)), merged[:, keep].astype(F32), merged_peer[...].astype(F32)
    ).astype(BF16)
    lanes = pl.ds(pl.multiple_of(pair * 128, 128), 128)
    own_half = merged_mine.at[mine]
    theirs = merged_mine.at[pl.ds(pl.multiple_of((1 - h) * HALF_V, HALF_V), HALF_V)]
    place = acts.at[h, pl.ds(pl.multiple_of(p * HALF_V, HALF_V), HALF_V), lanes]
    pltpu.make_async_copy(own_half, place, acts_recv).start()
    for step in (1, 3, 2, 0):
        if step > 0:
            remote(own_half, place, {"dep": along_y(step)}, acts_recv)
        remote(theirs, place, {"dep": along_y(step), "tp": 1 - h}, acts_recv)
    arrived(hop_a)
    hop_a = z_hop_a(3)
    arrived(ring)
    ring = ring_hop(TEXT, 3)
    text_spread(2, 6)
    arrived(hop_a)
    hop_a = z_hop_a(4)
    arrived(ring)
    ring = ring_hop(TEXT, 4)
    loads[4].wait()
    scaled = text_ref[...].astype(F32) * tgain_ref[...].reshape(1, 2 * QUARTER)
    text_chosen[h] = chosen_logits(scaled, router_ref[...].reshape(2 * QUARTER, 128), ids_ref[...])
    text_gates = remote(text_chosen.at[h], text_chosen.at[h], {"tp": 1 - h})
    for slot in range(NZ):
        plane_counts[pl.ds(lax.rem(z + slot, NZ), 1), :] = held_ids[slot, 2 * TOPK : 2 * TOPK + 1]
    all_counts[xy] = plane_counts[...]

    def send_counts(step, carry):
        pltpu.make_async_remote_copy(
            src_ref=plane_counts,
            dst_ref=all_counts.at[xy],
            send_sem=counts_send,
            recv_sem=counts_recv,
            device_id={"dep": z * PLANE + in_plane(step)},
            device_id_type=MESH,
        ).start()
        return carry

    lax.fori_loop(1, PLANE, send_counts, 0)
    arrived(hop_a)
    arrived(shared)
    pltpu.make_async_copy(acts, acts, acts_recv).wait()
    text_spread(3)

    def columns_of(zs):
        total = None
        for j in range(2):
            block = weights[j, pl.ds(zs, 2)].reshape(2 * NX * OWN_COLUMNS, V)
            product = jnp.dot(block, acts[j], preferred_element_type=F32)
            total = product if total is None else total + product
        return total

    vis_copies = []
    for c in range(2):
        vis_send[c] = columns_of((1 - h) * 4 + 2 * c)
        vis_copies.append(remote(vis_send.at[c], vis_recv.at[c], {"tp": 1 - h}))
    for c in range(2):
        product = columns_of(h * 4 + 2 * c)
        vis_copies[c].wait_recv()
        vis[pl.ds(8 * c, 8)] = (product + vis_recv[c]).astype(BF16).reshape(8, OWN_COLUMNS, 256)

    def vis_block(to_y):
        return vis.at[
            pl.ds(lax.rem(to_y, 2) * 8, 8), :, pl.ds(pl.multiple_of((to_y // 2) * 128, 128), 128)
        ]

    pltpu.make_async_copy(vis_block(y), vis_all.at[:, y], vis_all_recv).start()
    for step in range(1, NY):
        to_y = lax.rem(y + step, NY)
        remote(vis_block(to_y), vis_all.at[:, y], {"dep": along_y(step)}, vis_all_recv)
    text_spread(5)
    pltpu.make_async_copy(vis_all, vis_all, vis_all_recv).wait()

    hidden = vis_all[...].reshape(QUARTER, ROWS).astype(F32)
    me = p * 2 + h
    square_parts[me] = jnp.broadcast_to(jnp.sum(hidden * hidden, 0, keepdims=True), (8, ROWS))
    image_squares = to_unit(square_parts)
    arrived(ring)
    text_spread(4)
    image_rows[...] = hidden.T * tgain_ref[my_columns].reshape(1, QUARTER)
    arrived(image_squares)
    image_inverse = lax.rsqrt(total_of(square_parts)[0:1, :] / D + EPS)
    inverse = jnp.broadcast_to(image_inverse, (ROWS, ROWS)).T[:, 0:1]
    held[IMAGE, 0] = (image_rows[...] * inverse).astype(BF16)
    ring = ring_hop(IMAGE, 1)
    spread(IMAGE, 0)
    gate_parts[me] = chosen_logits(image_rows[...], router_ref[p], held_ids[0, TOPK : 2 * TOPK])
    image_gates = to_unit(gate_parts)
    for step in range(1, 5):
        arrived(ring)
        if step < 4:
            ring = ring_hop(IMAGE, step + 1)
        for slot in (step, NZ - step) if step < 4 else (4,):
            spread(IMAGE, slot)
    text_gates.wait_recv()
    arrived(image_gates)
    gate_ref[...] = jnp.where(
        flag((TOPK, ROWS)),
        gate(total_of(gate_parts) * image_inverse),
        gate((text_chosen[0] + text_chosen[1]) * text_inverse),
    )

    for copy in started:
        copy.wait_send()
    others = all_counts.at[pl.ds(0, PLANE - 1)]
    pltpu.make_async_copy(others, others, counts_send).wait()
    pltpu.make_async_copy(others, others, counts_recv).wait()
    lane = lax.broadcasted_iota(jnp.int32, (NZ, ROWS), 1)
    total_counts = jnp.zeros((NZ, ROWS), jnp.int32)
    for source in range(PLANE):
        total_counts += jnp.where(lane == source, all_counts[source], 0)
    counts_ref[...] = total_counts
    for phase in (TEXT, IMAGE):
        sent = stage.at[phase, :, pl.ds(0, (PLANE - 1) * SLOTS)]
        pltpu.make_async_copy(sent, sent, out_send.at[phase]).wait()
        pltpu.make_async_copy(outs[phase], outs[phase], out_recv.at[phase]).wait()


def fused(image_count, patches, text, ids, norms, proj, pout, merger, tgain, router):
    vmem = pl.BlockSpec(memory_space=pltpu.VMEM)
    hbm = pl.BlockSpec(memory_space=pl.ANY)
    loaded = (patches, text, proj, pout, merger, router)
    rows = NZ * PLANE // 2 * SLOTS
    buffer = pltpu.VMEM((rows, 2 * QUARTER), BF16)
    copies = 112
    return pl.pallas_call(
        fused_kernel,
        out_shape=(
            buffer,
            buffer,
            pltpu.VMEM((TOPK, ROWS), F32),
            pltpu.VMEM((NZ, ROWS), jnp.int32),
        ),
        in_specs=[pl.BlockSpec(memory_space=pltpu.SMEM), hbm, hbm]
        + [vmem] * 5
        + [hbm] * 3
        + [vmem, hbm],
        out_specs=(
            vmem,
            vmem,
            vmem,
            vmem,
        ),
        scratch_shapes=[pltpu.VMEM(a.shape, a.dtype) for a in loaded]
        + [
            pltpu.VMEM((4, V, 128), F32),
            pltpu.VMEM((V, PATCHES), BF16),
            pltpu.VMEM((V, PATCHES), BF16),
            pltpu.VMEM((HEADS, 128, PATCHES), BF16),
            pltpu.VMEM((HEADS, PATCHES, 128), BF16),
            pltpu.VMEM((HEADS, HEAD + 8, PATCHES), BF16),
            pltpu.VMEM((BAND, 256), F32),
            pltpu.VMEM((V, 256), F32),
            pltpu.VMEM((V, 256), F32),
            pltpu.VMEM((V, 256), BF16),
            pltpu.VMEM((V, 128), BF16),
            pltpu.VMEM((V, 128), BF16),
            pltpu.VMEM((2, V, 256), BF16),
            pltpu.VMEM((2, NZ, NX, OWN_COLUMNS, V), BF16),
            pltpu.VMEM((2, 256, 256), F32),
            pltpu.VMEM((2, 256, 256), F32),
            pltpu.VMEM((16, OWN_COLUMNS, 256), BF16),
            pltpu.VMEM((8, NY, OWN_COLUMNS, ROWS), BF16),
            pltpu.VMEM((ROWS, QUARTER), F32),
            pltpu.VMEM((ROWS, QUARTER), BF16),
            pltpu.VMEM((ROWS, 2 * QUARTER), BF16),
            pltpu.VMEM((2, 8, ROWS), F32),
            pltpu.VMEM((2, TOPK, ROWS), F32),
            pltpu.VMEM((TOPK, ROWS), jnp.int32),
            pltpu.VMEM((NZ, 2 * TOPK + 8, ROWS), jnp.int32),
            pltpu.VMEM((NZ, ROWS), jnp.int32),
            pltpu.VMEM((PLANE, NZ, ROWS), jnp.int32),
            pltpu.VMEM((2, NZ, ROWS, QUARTER), BF16),
            pltpu.VMEM((2, NZ, PLANE * SLOTS, QUARTER), BF16),
            pltpu.VMEM((4, 8, ROWS), F32),
            pltpu.VMEM((4, TOPK, ROWS), F32),
            pltpu.SemaphoreType.DMA((6,)),
            pltpu.SemaphoreType.DMA((copies,)),
            pltpu.SemaphoreType.DMA((copies,)),
            pltpu.SemaphoreType.DMA,
            pltpu.SemaphoreType.DMA,
            pltpu.SemaphoreType.DMA((2,)),
            pltpu.SemaphoreType.DMA((2,)),
            pltpu.SemaphoreType.DMA,
            pltpu.SemaphoreType.DMA,
        ],
        compiler_params=pltpu.CompilerParams(
            collective_id=0, has_side_effects=True, vmem_limit_bytes=46 * 1024 * 1024
        ),
    )(image_count, patches, text, ids, *norms, proj, pout, merger, tgain, router)


def interleave_kernel(counts_ref, text_ref, image_ref, gate_ref, out_ref, gate_out, sem):
    def pair_rows(ref, k):
        return ref.at[pl.ds(pl.multiple_of(k * SLOTS, SLOTS), SLOTS)]

    def step(k, carry):
        first = counts_ref[k // (PLANE // 2), 2 * lax.rem(k, PLANE // 2)]
        pltpu.make_async_copy(pair_rows(text_ref, k), pair_rows(out_ref, 2 * k + first), sem).start(
            priority=0
        )
        pltpu.make_async_copy(
            pair_rows(image_ref, k), pair_rows(out_ref, 2 * k + 1 - first), sem
        ).start(priority=1)
        return carry

    lax.fori_loop(0, NZ * PLANE // 2, step, 0)
    gate_out[...] = gate_ref[...]
    pltpu.make_async_copy(out_ref, out_ref, sem).wait()


def interleave(counts, text_rows, image_rows, gates):
    vmem = pl.BlockSpec(memory_space=pltpu.VMEM)
    held = pl.BlockSpec(memory_space=pl.ANY)
    return pl.pallas_call(
        interleave_kernel,
        out_shape=(
            jax.ShapeDtypeStruct((2 * text_rows.shape[0], text_rows.shape[1]), BF16),
            jax.ShapeDtypeStruct(gates.shape, F32),
        ),
        in_specs=[pl.BlockSpec(memory_space=pltpu.SMEM), held, held, vmem],
        out_specs=(held, vmem),
        scratch_shapes=[pltpu.SemaphoreType.DMA],
        compiler_params=pltpu.CompilerParams(vmem_limit_bytes=4 * 1024 * 1024),
    )(counts, text_rows, image_rows, gates)


def per_device(
    patches,
    image_count,
    text_tokens,
    norm_gain,
    norm_bias,
    patch_proj,
    patch_out,
    merge_gain,
    merge_bias,
    merger,
    token_gain,
    router,
    expert_ids,
):
    text_rows, image_rows, gates, counts = fused(
        image_count,
        patches.T,
        text_tokens,
        expert_ids.T,
        (norm_gain, norm_bias, merge_gain, merge_bias),
        patch_proj.transpose(1, 2, 0),
        patch_out,
        merger.transpose(0, 2, 1),
        token_gain,
        router.reshape(2, QUARTER, router.shape[1]),
    )
    dispatched, gate_probs = interleave(counts, text_rows, image_rows, gates)
    return dispatched[None], gate_probs.T


def solution(mesh):
    return jax.shard_map(
        per_device,
        mesh=mesh,
        in_specs=(
            P("dep", "tp"),
            P("dep"),
            P("dep", "tp"),
            P(),
            P(),
            P(None, None, "tp"),
            P("tp", None),
            P(),
            P(),
            P(None, "tp", "dep"),
            P("tp"),
            P("tp", None),
            P("dep", None),
        ),
        out_specs=(P("dep", None, "tp"), P("dep", None)),
        check_vma=False,
    )
```

```python
import math

import jax
import jax.numpy as jnp
from jax import lax
from jax.experimental import pallas as pl
from jax.experimental.pallas import tpu as pltpu
from jax.sharding import PartitionSpec as P

MESH = pl.DeviceIdType.MESH
BF16 = jnp.bfloat16
F32 = jnp.float32
NZ = 8
NX = 4
NY = 4
PLANE = NX * NY
SLOTS = 16
ROWS = 128
TOPK = 8
D = 4096
QUARTER = 1024
V = 1152
HALF_V = 576
PATCHES = 512
HEADS = 4
HEAD = 72
BAND = 288
OWN_COLUMNS = 32
EPS = 1e-06
TEXT = 0
IMAGE = 1


def selection(ids, first_expert):
    experts = first_expert + lax.broadcasted_iota(jnp.int32, (PLANE, ROWS), 0)
    count = jnp.zeros((PLANE, ROWS), F32)
    for k in range(TOPK):
        count += (ids[k : k + 1, :] == experts).astype(F32)
    earlier = (
        lax.broadcasted_iota(jnp.int32, (ROWS, ROWS), 0)
        < lax.broadcasted_iota(jnp.int32, (ROWS, ROWS), 1)
    ).astype(BF16)
    before = jnp.dot(count.astype(BF16), earlier, preferred_element_type=F32)
    slot = lax.broadcasted_iota(jnp.int32, (PLANE, SLOTS, ROWS), 1).astype(F32)
    first = before[:, None, :]
    last = (before + count)[:, None, :]
    chosen = (slot >= first) & (slot < last)
    return jnp.where(chosen, 1.0, 0.0).astype(BF16).reshape(PLANE * SLOTS, ROWS)


def fused_kernel(
    image_ref,
    patches_hbm,
    text_hbm,
    ids_ref,
    norm_gain_ref,
    norm_bias_ref,
    merge_gain_ref,
    merge_bias_ref,
    proj_hbm,
    pout_hbm,
    merger_hbm,
    tgain_ref,
    router_hbm,
    text_out,
    image_out,
    gate_ref,
    counts_ref,
    patches_ref,
    text_ref,
    proj_ref,
    pout_ref,
    merger_ref,
    router_ref,
    cols,
    pix,
    normed,
    qs,
    ks,
    vs,
    ctx,
    part_send,
    part_recv,
    merged,
    merged_peer,
    merged_mine,
    acts,
    weights,
    vis_send,
    vis_recv,
    vis,
    vis_all,
    image_rows,
    text_peer,
    text_normed,
    text_squares,
    text_chosen,
    ids_peer,
    held_ids,
    plane_counts,
    all_counts,
    held,
    stage,
    square_parts,
    gate_parts,
    load_sems,
    send_sems,
    recv_sems,
    acts_recv,
    vis_all_recv,
    out_send,
    out_recv,
    counts_send,
    counts_recv,
):
    dep = lax.axis_index("dep")
    h = lax.axis_index("tp")
    z = dep // PLANE
    xy = lax.rem(dep, PLANE)
    x = xy // NY
    y = lax.rem(xy, NY)
    pair = y // 2
    p = lax.rem(y, 2)
    outs = (text_out, image_out)

    def at(to_z, to_x, to_y):
        return to_z * PLANE + to_x * NY + to_y

    def along_z(step):
        return {"dep": at(lax.rem(z + NZ + step, NZ), x, y)}

    def along_x(step):
        return {"dep": at(z, lax.rem(x + NX + step, NX), y)}

    def along_y(step):
        return at(z, x, lax.rem(y + step, NY))

    def in_plane(step):
        mixed = lax.rem(7 * step, PLANE)
        to_x = lax.rem(x + mixed // NY, NX)
        to_y = lax.rem(y + lax.rem(mixed, NY), NY)
        return to_x * NY + to_y

    loads = []
    for n, (source, target) in enumerate(
        (
            (patches_hbm, patches_ref),
            (merger_hbm, merger_ref),
            (text_hbm, text_ref),
            (proj_hbm, proj_ref),
            (router_hbm, router_ref),
            (pout_hbm, pout_ref),
        )
    ):
        load = pltpu.make_async_copy(source, target, load_sems.at[n])
        load.start()
        loads.append(load)

    barrier = pltpu.get_barrier_semaphore()

    def greet(device):
        pl.semaphore_signal(barrier, inc=1, device_id=device, device_id_type=MESH)

    for step in range(1, NZ):
        greet(along_z(step))

    def greet_plane(step, carry):
        greet({"dep": z * PLANE + in_plane(step)})
        return carry

    lax.fori_loop(1, PLANE, greet_plane, 0)
    for step in range(NY):
        greet({"dep": along_y(step), "tp": 1 - h})

    other_chip = dep + 1 - 2 * p
    number = [0]
    started = []

    def remote(source, target, device, arrival=None):
        n = number[0]
        number[0] += 1
        copy = pltpu.make_async_remote_copy(
            src_ref=source,
            dst_ref=target,
            send_sem=send_sems.at[n],
            recv_sem=recv_sems.at[n] if arrival is None else arrival,
            device_id=device,
            device_id_type=MESH,
        )
        copy.start()
        started.append(copy)
        return copy

    def flag(shape):
        return jnp.full(shape, image_ref[0], jnp.int32) == 1

    row_from = lax.broadcasted_iota(jnp.int32, (PATCHES, PATCHES), 0)
    row_to = lax.broadcasted_iota(jnp.int32, (PATCHES, PATCHES), 1)
    order = jnp.where(
        row_from == 4 * lax.rem(row_to, ROWS) + row_to // ROWS, 1.0, 0.0
    ).astype(BF16)
    mine = pl.ds(pl.multiple_of(h * HALF_V, HALF_V), HALF_V)
    loads[0].wait()
    pix[mine, :] = jnp.dot(patches_ref[...], order, preferred_element_type=F32).astype(BF16)
    loads[1].wait()
    for j in range(2):
        weights[j, z, x] = jnp.concatenate([merger_ref[2 * j], merger_ref[2 * j + 1]], 1)
    loads[2].wait()
    raw = text_ref[...].astype(F32)
    squares = jnp.broadcast_to(jnp.sum(raw * raw, 1, keepdims=True), (ROWS, ROWS))
    text_squares[h] = jnp.broadcast_to(squares.T[0:1, :], (8, ROWS))

    pl.semaphore_wait(barrier, NZ - 1 + PLANE - 1 + NY)

    text_columns = pl.ds(pl.multiple_of((1 - p) * QUARTER, QUARTER), QUARTER)
    my_columns = pl.ds(pl.multiple_of(p * QUARTER, QUARTER), QUARTER)
    squares_copy = remote(text_squares.at[h], text_squares.at[h], {"tp": 1 - h})
    pix_copy = remote(pix.at[mine], pix.at[mine], {"tp": 1 - h})
    ids_copy = remote(ids_ref, ids_peer, {"dep": other_chip})
    across_x = [
        remote(weights.at[0, z, x], weights.at[0, z, x], along_x(step)) for step in (1, 3, 2)
    ]

    def both_ways(right, left, along):
        return (
            remote(right, right, along(1)),
            remote(left, left, along(-1)),
        )

    def z_hop_a(step):
        back, ahead = lax.rem(z + NZ + 1 - step, NZ), lax.rem(z + step - 1, NZ)
        right = pl.ds(0, 4 if step < 4 else 2)
        left = right if step < 4 else pl.ds(2, 2)
        return both_ways(weights.at[0, back, right], weights.at[0, ahead, left], along_z)

    def z_hop_b(step):
        back, ahead = lax.rem(z + NZ + 1 - step, NZ), lax.rem(z + step - 1, NZ)
        right = pl.ds(0, OWN_COLUMNS if step < 4 else OWN_COLUMNS // 2)
        left = right if step < 4 else pl.ds(OWN_COLUMNS // 2, OWN_COLUMNS // 2)
        return both_ways(weights.at[1, back, x, right], weights.at[1, ahead, x, left], along_z)

    def arrived(copies):
        for copy in copies:
            copy.wait_recv()

    def x_send_b(*blocks):
        for block in blocks:
            to_share = weights.at[1, lax.rem(z + NZ + block, NZ), x]
            for step in (1, 3, 2):
                shared.append(remote(to_share, to_share, along_x(step)))

    shared = []
    hop_b = z_hop_b(1)
    x_send_b(0)

    squares_copy.wait_recv()
    text_inverse = lax.rsqrt((text_squares[0] + text_squares[1]) / D + EPS)[0:1, :]
    inverse = jnp.broadcast_to(text_inverse, (ROWS, ROWS)).T[:, 0:1]
    text_normed[...] = (
        text_ref[...].astype(F32) * tgain_ref[...].reshape(1, 2 * QUARTER) * inverse
    ).astype(BF16)
    text_copy = remote(text_normed.at[:, text_columns], text_peer, {"dep": other_chip})

    for v, vector in enumerate((norm_gain_ref, norm_bias_ref, merge_gain_ref, merge_bias_ref)):
        for c in range(0, V, 128):
            row = jnp.broadcast_to(vector[c : c + 128].reshape(1, 128), (128, 128))
            cols[v, c : c + 128, :] = row.T

    def layer_norm(values, gain, bias):
        mean = jnp.sum(values, 0, keepdims=True) / V
        variance = jnp.sum(values * values, 0, keepdims=True) / V - mean * mean
        return (values - mean) * lax.rsqrt(variance + EPS) * gain + bias

    def to_unit(parts):
        me = p * 2 + h
        return [
            remote(
                parts.at[me],
                parts.at[me],
                {"dep": dep if dp == 0 else other_chip, "tp": h if dh == 0 else 1 - h},
            )
            for dp, dh in ((0, 1), (1, 0), (1, 1))
        ]

    def total_of(parts):
        return parts[0] + parts[1] + parts[2] + parts[3]

    def chosen_logits(scaled, weight, ids):
        logits = jnp.dot(scaled.astype(BF16), weight, preferred_element_type=F32).T
        expert = lax.broadcasted_iota(jnp.int32, (128, ROWS), 0)
        return jnp.concatenate(
            [
                jnp.sum(jnp.where(ids[k : k + 1, :] == expert, logits, 0.0), 0, keepdims=True)
                for k in range(TOPK)
            ],
            0,
        )

    def gate(chosen):
        raised = jnp.exp(chosen - jnp.max(chosen, 0, keepdims=True))
        return raised / jnp.sum(raised, 0, keepdims=True)

    def ring_hop(phase, step):
        back, ahead = lax.rem(NZ + 1 - step, NZ), step - 1
        right = pl.ds(0, QUARTER if step < 4 else QUARTER // 2)
        left = right if step < 4 else pl.ds(QUARTER // 2, QUARTER // 2)
        return (
            remote(
                held.at[phase, back, :, right], held.at[phase, NZ - step, :, right], along_z(1)
            ),
            remote(
                held.at[phase, ahead, :, left], held.at[phase, step, :, left], along_z(NZ - 1)
            ),
        )

    def spread(phase, slot):
        ids = held_ids[slot, phase * TOPK : (phase + 1) * TOPK]
        chosen = selection(ids, z * PLANE)
        for c in range(0, QUARTER, 512):
            stage[phase, slot, :, c : c + 512] = jnp.dot(
                chosen, held[phase, slot, :, c : c + 512], preferred_element_type=F32
            ).astype(BF16)
        source_pair = lax.rem(z + slot, NZ) * (PLANE // 2) + xy // 2
        at_dest = outs[phase].at[pl.ds(source_pair * SLOTS, SLOTS), my_columns]
        pltpu.make_async_copy(
            stage.at[phase, slot, pl.ds(xy * SLOTS, SLOTS)], at_dest, out_recv.at[phase]
        ).start()

        def send(step, carry):
            peer = in_plane(step)
            pltpu.make_async_remote_copy(
                src_ref=stage.at[phase, slot, pl.ds(peer * SLOTS, SLOTS)],
                dst_ref=at_dest,
                send_sem=out_send.at[phase],
                recv_sem=out_recv.at[phase],
                device_id={"dep": z * PLANE + peer},
                device_id_type=MESH,
            ).start()
            return carry

        lax.fori_loop(1, PLANE, send, 0)

    def text_spread(*slots):
        for slot in slots:
            spread(TEXT, slot)

    def attend(lanes):
        for head in range(HEADS):
            scores = jnp.dot(ks[head], qs[head, :, lanes], preferred_element_type=F32)
            below = scores - jnp.max(scores, 0, keepdims=True)
            raised = jnp.exp2(below * (math.log2(math.e) / math.sqrt(HEAD))).astype(BF16)
            product = jnp.dot(vs[head], raised, preferred_element_type=F32)
            ctx[head * HEAD : (head + 1) * HEAD, :] = product[:HEAD] / product[HEAD : HEAD + 1]
        return ctx[...].astype(BF16)

    def out_product(context, lo):
        return lax.dot_general(
            pout_ref[:, lo : lo + 384],
            context,
            (((0,), (0,)), ((), ())),
            preferred_element_type=F32,
        )

    pix_copy.wait_recv()
    for c in range(0, PATCHES, 128):
        normed[:, c : c + 128] = layer_norm(
            pix[:, c : c + 128].astype(F32), cols[0], cols[1]
        ).astype(BF16)
    loads[3].wait()
    pad = jnp.zeros((128 - HEAD, PATCHES), F32)
    queries = jnp.dot(proj_ref[0], normed[...], preferred_element_type=F32)
    for head in range(HEADS):
        part = jnp.concatenate([queries[head * HEAD : (head + 1) * HEAD], pad], 0)
        qs[head] = part.astype(BF16)
    keys = jnp.dot(proj_ref[1], normed[...], preferred_element_type=F32)
    for head in range(HEADS):
        part = jnp.concatenate([keys[head * HEAD : (head + 1) * HEAD], pad], 0)
        ks[head] = part.T.astype(BF16)
    values = jnp.dot(proj_ref[2], normed[...], preferred_element_type=F32)
    ones = jnp.ones((8, PATCHES), F32)
    for head in range(HEADS):
        part = jnp.concatenate([values[head * HEAD : (head + 1) * HEAD], ones], 0)
        vs[head] = part.astype(BF16)

    ids_copy.wait_recv()
    has = flag((TOPK, ROWS))
    held_ids[0, 0:TOPK] = jnp.where(has, ids_peer[...], ids_ref[...])
    held_ids[0, TOPK : 2 * TOPK] = jnp.where(has, ids_ref[...], ids_peer[...])
    held_ids[0, 2 * TOPK :] = jnp.full((8, ROWS), image_ref[0], jnp.int32)
    id_copies = [
        remote(held_ids.at[0], held_ids.at[NZ - step], along_z(step)) for step in range(1, NZ)
    ]

    my_rows = pl.ds(pl.multiple_of(h * 256, 256), 256)
    their_rows = pl.ds(pl.multiple_of((1 - h) * 256, 256), 256)
    arrived(hop_b)
    hop_b = z_hop_b(2)
    x_send_b(1, -1)
    arrived(across_x)
    hop_a = z_hop_a(1)
    context = attend(their_rows)
    loads[5].wait()
    part_copies = []
    for lo in range(0, V, 384):
        part_send[lo : lo + 384, :] = out_product(context, lo)
        block = pl.ds(lo, 384)
        part_copies.append(remote(part_send.at[block], part_recv.at[block], {"tp": 1 - h}))
    text_copy.wait_recv()
    held[TEXT, 0] = jnp.where(
        flag((ROWS, QUARTER)), text_peer[...].astype(F32), text_normed[:, my_columns].astype(F32)
    ).astype(BF16)
    ring = ring_hop(TEXT, 1)
    text_spread(0)
    context = attend(my_rows)
    arrived(hop_b)
    hop_b = z_hop_b(3)
    x_send_b(2, -2)
    arrived(part_copies)
    for lo in range(0, V, 384):
        block = pl.ds(lo, 384)
        part_recv[block, :] += out_product(context, lo) + pix[block, my_rows].astype(F32)
    for c in range(0, 256, 128):
        merged[:, c : c + 128] = layer_norm(part_recv[:, c : c + 128], cols[2], cols[3]).astype(
            BF16
        )
    keep = pl.ds(pl.multiple_of(p * 128, 128), 128)
    give = pl.ds(pl.multiple_of((1 - p) * 128, 128), 128)
    merged_copy = remote(merged.at[:, give], merged_peer, {"dep": other_chip})

    arrived(hop_b)
    hop_b = z_hop_b(4)
    x_send_b(3, -3)
    arrived(hop_a)
    hop_a = z_hop_a(2)
    arrived(ring)
    arrived(id_copies)
    text_spread(1, 7)
    arrived(hop_b)
    x_send_b(4)
    merged_copy.wait_recv()
    merged_mine[...] = jnp.where(
        flag((V, 128)), merged[:, keep].astype(F32), merged_peer[...].astype(F32)
    ).astype(BF16)
    lanes = pl.ds(pl.multiple_of(pair * 128, 128), 128)
    own_half = merged_mine.at[mine]
    theirs = merged_mine.at[pl.ds(pl.multiple_of((1 - h) * HALF_V, HALF_V), HALF_V)]
    place = acts.at[h, pl.ds(pl.multiple_of(p * HALF_V, HALF_V), HALF_V), lanes]
    pltpu.make_async_copy(own_half, place, acts_recv).start()
    for step in (1, 3, 2, 0):
        if step > 0:
            remote(own_half, place, {"dep": along_y(step)}, acts_recv)
        remote(theirs, place, {"dep": along_y(step), "tp": 1 - h}, acts_recv)
    arrived(hop_a)
    hop_a = z_hop_a(3)
    ring = ring_hop(TEXT, 2)
    arrived(hop_a)
    hop_a = z_hop_a(4)
    arrived(ring)
    ring = ring_hop(TEXT, 3)
    text_spread(2)
    loads[4].wait()
    scaled = text_ref[...].astype(F32) * tgain_ref[...].reshape(1, 2 * QUARTER)
    text_chosen[h] = chosen_logits(scaled, router_ref[...].reshape(2 * QUARTER, 128), ids_ref[...])
    text_gates = remote(text_chosen.at[h], text_chosen.at[h], {"tp": 1 - h})
    for slot in range(NZ):
        plane_counts[pl.ds(lax.rem(z + slot, NZ), 1), :] = held_ids[slot, 2 * TOPK : 2 * TOPK + 1]
    all_counts[xy] = plane_counts[...]

    def send_counts(step, carry):
        pltpu.make_async_remote_copy(
            src_ref=plane_counts,
            dst_ref=all_counts.at[xy],
            send_sem=counts_send,
            recv_sem=counts_recv,
            device_id={"dep": z * PLANE + in_plane(step)},
            device_id_type=MESH,
        ).start()
        return carry

    lax.fori_loop(1, PLANE, send_counts, 0)
    arrived(hop_a)
    arrived(shared)
    pltpu.make_async_copy(acts, acts, acts_recv).wait()
    text_spread(6)

    def columns_of(zs):
        total = None
        for j in range(2):
            block = weights[j, pl.ds(zs, 2)].reshape(2 * NX * OWN_COLUMNS, V)
            product = jnp.dot(block, acts[j], preferred_element_type=F32)
            total = product if total is None else total + product
        return total

    vis_copies = []
    for c in range(2):
        vis_send[c] = columns_of((1 - h) * 4 + 2 * c)
        vis_copies.append(remote(vis_send.at[c], vis_recv.at[c], {"tp": 1 - h}))
    squares = jnp.zeros((1, 2 * ROWS), F32)
    for c in range(2):
        product = columns_of(h * 4 + 2 * c)
        vis_copies[c].wait_recv()
        rounded = (product + vis_recv[c]).astype(BF16)
        vis[pl.ds(8 * c, 8)] = rounded.reshape(8, OWN_COLUMNS, 256)
        rounded = rounded.astype(F32)
        squares = squares + jnp.sum(rounded * rounded, 0, keepdims=True)
    core = 2 * y + h
    square_parts[core] = jnp.broadcast_to(squares, (8, 2 * ROWS))
    image_squares = [
        remote(
            square_parts.at[core],
            square_parts.at[core],
            {"dep": along_y(dy), "tp": h if dh == 0 else 1 - h},
        )
        for dy in range(NY)
        for dh in range(2)
        if dy + dh > 0
    ]

    def vis_block(to_y):
        return vis.at[
            pl.ds(lax.rem(to_y, 2) * 8, 8), :, pl.ds(pl.multiple_of((to_y // 2) * 128, 128), 128)
        ]

    pltpu.make_async_copy(vis_block(y), vis_all.at[:, y], vis_all_recv).start()
    for step in range(1, NY):
        to_y = lax.rem(y + step, NY)
        remote(vis_block(to_y), vis_all.at[:, y], {"dep": along_y(step)}, vis_all_recv)
    arrived(ring)
    ring = ring_hop(TEXT, 4)
    text_spread(3, 5)
    pltpu.make_async_copy(vis_all, vis_all, vis_all_recv).wait()

    hidden = vis_all[...].reshape(QUARTER, ROWS).astype(F32)
    me = p * 2 + h
    image_rows[...] = hidden.T * tgain_ref[my_columns].reshape(1, QUARTER)
    arrived(image_squares)
    squares = sum(square_parts[core, 0:1, lanes] for core in range(2 * NY))
    image_inverse = lax.rsqrt(squares / D + EPS)
    inverse = jnp.broadcast_to(image_inverse, (ROWS, ROWS)).T[:, 0:1]
    held[IMAGE, 0] = (image_rows[...] * inverse).astype(BF16)
    last_text = ring
    ring = ring_hop(IMAGE, 1)
    spread(IMAGE, 0)
    arrived(last_text)
    text_spread(4)
    gate_parts[me] = chosen_logits(image_rows[...], router_ref[p], held_ids[0, TOPK : 2 * TOPK])
    image_gates = to_unit(gate_parts)
    for step in range(1, 5):
        arrived(ring)
        if step < 4:
            ring = ring_hop(IMAGE, step + 1)
        for slot in (step, NZ - step) if step < 4 else (4,):
            spread(IMAGE, slot)
    text_gates.wait_recv()
    arrived(image_gates)
    gate_ref[...] = jnp.where(
        flag((TOPK, ROWS)),
        gate(total_of(gate_parts) * image_inverse),
        gate((text_chosen[0] + text_chosen[1]) * text_inverse),
    )

    for copy in started:
        copy.wait_send()
    others = all_counts.at[pl.ds(0, PLANE - 1)]
    pltpu.make_async_copy(others, others, counts_send).wait()
    pltpu.make_async_copy(others, others, counts_recv).wait()
    lane = lax.broadcasted_iota(jnp.int32, (NZ, ROWS), 1)
    total_counts = jnp.zeros((NZ, ROWS), jnp.int32)
    for source in range(PLANE):
        total_counts += jnp.where(lane == source, all_counts[source], 0)
    counts_ref[...] = total_counts
    for phase in (TEXT, IMAGE):
        sent = stage.at[phase, :, pl.ds(0, (PLANE - 1) * SLOTS)]
        pltpu.make_async_copy(sent, sent, out_send.at[phase]).wait()
        pltpu.make_async_copy(outs[phase], outs[phase], out_recv.at[phase]).wait()


def fused(image_count, patches, text, ids, norms, proj, pout, merger, tgain, router):
    vmem = pl.BlockSpec(memory_space=pltpu.VMEM)
    hbm = pl.BlockSpec(memory_space=pl.ANY)
    loaded = (patches, text, proj, pout, merger, router)
    rows = NZ * PLANE // 2 * SLOTS
    buffer = pltpu.VMEM((rows, 2 * QUARTER), BF16)
    copies = 128
    return pl.pallas_call(
        fused_kernel,
        out_shape=(
            buffer,
            buffer,
            pltpu.VMEM((TOPK, ROWS), F32),
            pltpu.VMEM((NZ, ROWS), jnp.int32),
        ),
        in_specs=[pl.BlockSpec(memory_space=pltpu.SMEM), hbm, hbm]
        + [vmem] * 5
        + [hbm] * 3
        + [vmem, hbm],
        out_specs=(
            vmem,
            vmem,
            vmem,
            vmem,
        ),
        scratch_shapes=[pltpu.VMEM(a.shape, a.dtype) for a in loaded]
        + [
            pltpu.VMEM((4, V, 128), F32),
            pltpu.VMEM((V, PATCHES), BF16),
            pltpu.VMEM((V, PATCHES), BF16),
            pltpu.VMEM((HEADS, 128, PATCHES), BF16),
            pltpu.VMEM((HEADS, PATCHES, 128), BF16),
            pltpu.VMEM((HEADS, HEAD + 8, PATCHES), BF16),
            pltpu.VMEM((BAND, 256), F32),
            pltpu.VMEM((V, 256), F32),
            pltpu.VMEM((V, 256), F32),
            pltpu.VMEM((V, 256), BF16),
            pltpu.VMEM((V, 128), BF16),
            pltpu.VMEM((V, 128), BF16),
            pltpu.VMEM((2, V, 256), BF16),
            pltpu.VMEM((2, NZ, NX, OWN_COLUMNS, V), BF16),
            pltpu.VMEM((2, 256, 256), F32),
            pltpu.VMEM((2, 256, 256), F32),
            pltpu.VMEM((16, OWN_COLUMNS, 256), BF16),
            pltpu.VMEM((8, NY, OWN_COLUMNS, ROWS), BF16),
            pltpu.VMEM((ROWS, QUARTER), F32),
            pltpu.VMEM((ROWS, QUARTER), BF16),
            pltpu.VMEM((ROWS, 2 * QUARTER), BF16),
            pltpu.VMEM((2, 8, ROWS), F32),
            pltpu.VMEM((2, TOPK, ROWS), F32),
            pltpu.VMEM((TOPK, ROWS), jnp.int32),
            pltpu.VMEM((NZ, 2 * TOPK + 8, ROWS), jnp.int32),
            pltpu.VMEM((NZ, ROWS), jnp.int32),
            pltpu.VMEM((PLANE, NZ, ROWS), jnp.int32),
            pltpu.VMEM((2, NZ, ROWS, QUARTER), BF16),
            pltpu.VMEM((2, NZ, PLANE * SLOTS, QUARTER), BF16),
            pltpu.VMEM((2 * NY, 8, 2 * ROWS), F32),
            pltpu.VMEM((4, TOPK, ROWS), F32),
            pltpu.SemaphoreType.DMA((6,)),
            pltpu.SemaphoreType.DMA((copies,)),
            pltpu.SemaphoreType.DMA((copies,)),
            pltpu.SemaphoreType.DMA,
            pltpu.SemaphoreType.DMA,
            pltpu.SemaphoreType.DMA((2,)),
            pltpu.SemaphoreType.DMA((2,)),
            pltpu.SemaphoreType.DMA,
            pltpu.SemaphoreType.DMA,
        ],
        compiler_params=pltpu.CompilerParams(
            collective_id=0, has_side_effects=True, vmem_limit_bytes=46 * 1024 * 1024
        ),
    )(image_count, patches, text, ids, *norms, proj, pout, merger, tgain, router)


def interleave_kernel(counts_ref, text_ref, image_ref, gate_ref, out_ref, gate_out, sem):
    def pair_rows(ref, k):
        return ref.at[pl.ds(pl.multiple_of(k * SLOTS, SLOTS), SLOTS)]

    def step(k, carry):
        first = counts_ref[k // (PLANE // 2), 2 * lax.rem(k, PLANE // 2)]
        pltpu.make_async_copy(pair_rows(text_ref, k), pair_rows(out_ref, 2 * k + first), sem).start(
            priority=0
        )
        pltpu.make_async_copy(
            pair_rows(image_ref, k), pair_rows(out_ref, 2 * k + 1 - first), sem
        ).start(priority=1)
        return carry

    lax.fori_loop(0, NZ * PLANE // 2, step, 0)
    gate_out[...] = gate_ref[...]
    pltpu.make_async_copy(out_ref, out_ref, sem).wait()


def interleave(counts, text_rows, image_rows, gates):
    vmem = pl.BlockSpec(memory_space=pltpu.VMEM)
    held = pl.BlockSpec(memory_space=pl.ANY)
    return pl.pallas_call(
        interleave_kernel,
        out_shape=(
            jax.ShapeDtypeStruct((2 * text_rows.shape[0], text_rows.shape[1]), BF16),
            jax.ShapeDtypeStruct(gates.shape, F32),
        ),
        in_specs=[pl.BlockSpec(memory_space=pltpu.SMEM), held, held, vmem],
        out_specs=(held, vmem),
        scratch_shapes=[pltpu.SemaphoreType.DMA],
        compiler_params=pltpu.CompilerParams(vmem_limit_bytes=4 * 1024 * 1024),
    )(counts, text_rows, image_rows, gates)


def per_device(
    patches,
    image_count,
    text_tokens,
    norm_gain,
    norm_bias,
    patch_proj,
    patch_out,
    merge_gain,
    merge_bias,
    merger,
    token_gain,
    router,
    expert_ids,
):
    text_rows, image_rows, gates, counts = fused(
        image_count,
        patches.T,
        text_tokens,
        expert_ids.T,
        (norm_gain, norm_bias, merge_gain, merge_bias),
        patch_proj.transpose(1, 2, 0),
        patch_out,
        merger.transpose(0, 2, 1),
        token_gain,
        router.reshape(2, QUARTER, router.shape[1]),
    )
    dispatched, gate_probs = interleave(counts, text_rows, image_rows, gates)
    return dispatched[None], gate_probs.T


def solution(mesh):
    return jax.shard_map(
        per_device,
        mesh=mesh,
        in_specs=(
            P("dep", "tp"),
            P("dep"),
            P("dep", "tp"),
            P(),
            P(),
            P(None, None, "tp"),
            P("tp", None),
            P(),
            P(),
            P(None, "tp", "dep"),
            P("tp"),
            P("tp", None),
            P("dep", None),
        ),
        out_specs=(P("dep", None, "tp"), P("dep", None)),
        check_vma=False,
    )
```

```python
import math

import jax
import jax.numpy as jnp
from jax import lax
from jax.experimental import pallas as pl
from jax.experimental.pallas import tpu as pltpu
from jax.sharding import PartitionSpec as P

MESH = pl.DeviceIdType.MESH
BF16 = jnp.bfloat16
F32 = jnp.float32
NZ = 8
NX = 4
NY = 4
PLANE = NX * NY
SLOTS = 16
ROWS = 128
TOPK = 8
D = 4096
QUARTER = 1024
V = 1152
HALF_V = 576
PATCHES = 512
HEADS = 4
HEAD = 72
BAND = 288
OWN_COLUMNS = 32
EPS = 1e-06
TEXT = 0
IMAGE = 1


def selection(ids, first_expert):
    experts = first_expert + lax.broadcasted_iota(jnp.int32, (PLANE, ROWS), 0)
    count = jnp.zeros((PLANE, ROWS), F32)
    for k in range(TOPK):
        count += (ids[k : k + 1, :] == experts).astype(F32)
    earlier = (
        lax.broadcasted_iota(jnp.int32, (ROWS, ROWS), 0)
        < lax.broadcasted_iota(jnp.int32, (ROWS, ROWS), 1)
    ).astype(BF16)
    before = jnp.dot(count.astype(BF16), earlier, preferred_element_type=F32)
    slot = lax.broadcasted_iota(jnp.int32, (PLANE, SLOTS, ROWS), 1).astype(F32)
    first = before[:, None, :]
    last = (before + count)[:, None, :]
    chosen = (slot >= first) & (slot < last)
    return jnp.where(chosen, 1.0, 0.0).astype(BF16).reshape(PLANE * SLOTS, ROWS)


def fused_kernel(
    image_ref,
    patches_hbm,
    text_hbm,
    ids_ref,
    norm_gain_ref,
    norm_bias_ref,
    merge_gain_ref,
    merge_bias_ref,
    proj_hbm,
    pout_hbm,
    merger_hbm,
    tgain_ref,
    router_hbm,
    text_out,
    image_out,
    gate_ref,
    counts_ref,
    patches_ref,
    text_ref,
    proj_ref,
    pout_ref,
    merger_ref,
    router_ref,
    cols,
    pix,
    normed,
    qs,
    ks,
    vs,
    ctx,
    part_send,
    part_recv,
    merged,
    merged_peer,
    merged_mine,
    acts,
    weights,
    vis_send,
    vis_recv,
    vis,
    vis_all,
    image_rows,
    text_peer,
    text_normed,
    text_squares,
    text_chosen,
    ids_peer,
    held_ids,
    plane_counts,
    all_counts,
    held,
    stage,
    square_parts,
    gate_parts,
    load_sems,
    send_sems,
    recv_sems,
    acts_recv,
    vis_all_recv,
    out_send,
    out_recv,
    counts_send,
    counts_recv,
):
    dep = lax.axis_index("dep")
    h = lax.axis_index("tp")
    z = dep // PLANE
    xy = lax.rem(dep, PLANE)
    x = xy // NY
    y = lax.rem(xy, NY)
    pair = y // 2
    p = lax.rem(y, 2)
    outs = (text_out, image_out)

    def at(to_z, to_x, to_y):
        return to_z * PLANE + to_x * NY + to_y

    def along_z(step):
        return {"dep": at(lax.rem(z + NZ + step, NZ), x, y)}

    def along_x(step):
        return {"dep": at(z, lax.rem(x + NX + step, NX), y)}

    def along_y(step):
        return at(z, x, lax.rem(y + step, NY))

    def in_plane(step):
        mixed = lax.rem(7 * step, PLANE)
        to_x = lax.rem(x + mixed // NY, NX)
        to_y = lax.rem(y + lax.rem(mixed, NY), NY)
        return to_x * NY + to_y

    loads = []
    for n, (source, target) in enumerate(
        (
            (patches_hbm, patches_ref),
            (merger_hbm, merger_ref),
            (text_hbm, text_ref),
            (proj_hbm, proj_ref),
            (router_hbm, router_ref),
            (pout_hbm, pout_ref),
        )
    ):
        load = pltpu.make_async_copy(source, target, load_sems.at[n])
        load.start()
        loads.append(load)

    barrier = pltpu.get_barrier_semaphore()

    def greet(device):
        pl.semaphore_signal(barrier, inc=1, device_id=device, device_id_type=MESH)

    for step in range(1, NZ):
        greet(along_z(step))

    def greet_plane(step, carry):
        greet({"dep": z * PLANE + in_plane(step)})
        return carry

    lax.fori_loop(1, PLANE, greet_plane, 0)
    for step in range(NY):
        greet({"dep": along_y(step), "tp": 1 - h})

    other_chip = dep + 1 - 2 * p
    number = [0]
    started = []

    def remote(source, target, device, arrival=None):
        n = number[0]
        number[0] += 1
        copy = pltpu.make_async_remote_copy(
            src_ref=source,
            dst_ref=target,
            send_sem=send_sems.at[n],
            recv_sem=recv_sems.at[n] if arrival is None else arrival,
            device_id=device,
            device_id_type=MESH,
        )
        copy.start()
        started.append(copy)
        return copy

    def flag(shape):
        return jnp.full(shape, image_ref[0], jnp.int32) == 1

    row_from = lax.broadcasted_iota(jnp.int32, (PATCHES, PATCHES), 0)
    row_to = lax.broadcasted_iota(jnp.int32, (PATCHES, PATCHES), 1)
    order = jnp.where(
        row_from == 4 * lax.rem(row_to, ROWS) + row_to // ROWS, 1.0, 0.0
    ).astype(BF16)
    mine = pl.ds(pl.multiple_of(h * HALF_V, HALF_V), HALF_V)
    loads[0].wait()
    pix[mine, :] = jnp.dot(patches_ref[...], order, preferred_element_type=F32).astype(BF16)
    loads[1].wait()
    for j in range(2):
        weights[j, z, x] = jnp.concatenate([merger_ref[2 * j], merger_ref[2 * j + 1]], 1)
    loads[2].wait()
    raw = text_ref[...].astype(F32)
    squares = jnp.broadcast_to(jnp.sum(raw * raw, 1, keepdims=True), (ROWS, ROWS))
    text_squares[h] = jnp.broadcast_to(squares.T[0:1, :], (8, ROWS))

    pl.semaphore_wait(barrier, NZ - 1 + PLANE - 1 + NY)

    text_columns = pl.ds(pl.multiple_of((1 - p) * QUARTER, QUARTER), QUARTER)
    my_columns = pl.ds(pl.multiple_of(p * QUARTER, QUARTER), QUARTER)
    squares_copy = remote(text_squares.at[h], text_squares.at[h], {"tp": 1 - h})
    pix_copy = remote(pix.at[mine], pix.at[mine], {"tp": 1 - h})
    ids_copy = remote(ids_ref, ids_peer, {"dep": other_chip})
    across_x = [
        remote(weights.at[0, z, x], weights.at[0, z, x], along_x(step)) for step in (1, 3, 2)
    ]

    def both_ways(right, left, along):
        return (
            remote(right, right, along(1)),
            remote(left, left, along(-1)),
        )

    def z_hop_a(step):
        back, ahead = lax.rem(z + NZ + 1 - step, NZ), lax.rem(z + step - 1, NZ)
        right = pl.ds(0, 4 if step < 4 else 2)
        left = right if step < 4 else pl.ds(2, 2)
        return both_ways(weights.at[0, back, right], weights.at[0, ahead, left], along_z)

    def z_hop_b(step):
        back, ahead = lax.rem(z + NZ + 1 - step, NZ), lax.rem(z + step - 1, NZ)
        right = pl.ds(0, OWN_COLUMNS if step < 4 else OWN_COLUMNS // 2)
        left = right if step < 4 else pl.ds(OWN_COLUMNS // 2, OWN_COLUMNS // 2)
        return both_ways(weights.at[1, back, x, right], weights.at[1, ahead, x, left], along_z)

    def arrived(copies):
        for copy in copies:
            copy.wait_recv()

    def x_send_b(*blocks):
        for block in blocks:
            to_share = weights.at[1, lax.rem(z + NZ + block, NZ), x]
            for step in (1, 3, 2):
                shared.append(remote(to_share, to_share, along_x(step)))

    shared = []
    hop_b = z_hop_b(1)
    x_send_b(0)

    squares_copy.wait_recv()
    text_inverse = lax.rsqrt((text_squares[0] + text_squares[1]) / D + EPS)[0:1, :]
    inverse = jnp.broadcast_to(text_inverse, (ROWS, ROWS)).T[:, 0:1]
    text_normed[...] = (
        text_ref[...].astype(F32) * tgain_ref[...].reshape(1, 2 * QUARTER) * inverse
    ).astype(BF16)
    text_copy = remote(text_normed.at[:, text_columns], text_peer, {"dep": other_chip})

    for v, vector in enumerate((norm_gain_ref, norm_bias_ref, merge_gain_ref, merge_bias_ref)):
        for c in range(0, V, 128):
            row = jnp.broadcast_to(vector[c : c + 128].reshape(1, 128), (128, 128))
            cols[v, c : c + 128, :] = row.T

    def layer_norm(values, gain, bias):
        mean = jnp.sum(values, 0, keepdims=True) / V
        variance = jnp.sum(values * values, 0, keepdims=True) / V - mean * mean
        return (values - mean) * lax.rsqrt(variance + EPS) * gain + bias

    def to_unit(parts):
        me = p * 2 + h
        return [
            remote(
                parts.at[me],
                parts.at[me],
                {"dep": dep if dp == 0 else other_chip, "tp": h if dh == 0 else 1 - h},
            )
            for dp, dh in ((0, 1), (1, 0), (1, 1))
        ]

    def total_of(parts):
        return parts[0] + parts[1] + parts[2] + parts[3]

    def chosen_logits(scaled, weight, ids):
        logits = jnp.dot(scaled.astype(BF16), weight, preferred_element_type=F32).T
        expert = lax.broadcasted_iota(jnp.int32, (128, ROWS), 0)
        return jnp.concatenate(
            [
                jnp.sum(jnp.where(ids[k : k + 1, :] == expert, logits, 0.0), 0, keepdims=True)
                for k in range(TOPK)
            ],
            0,
        )

    def gate(chosen):
        raised = jnp.exp(chosen - jnp.max(chosen, 0, keepdims=True))
        return raised / jnp.sum(raised, 0, keepdims=True)

    def ring_hop(phase, step):
        back, ahead = lax.rem(NZ + 1 - step, NZ), step - 1
        right = pl.ds(0, QUARTER if step < 4 else QUARTER // 2)
        left = right if step < 4 else pl.ds(QUARTER // 2, QUARTER // 2)
        return (
            remote(
                held.at[phase, back, :, right], held.at[phase, NZ - step, :, right], along_z(1)
            ),
            remote(
                held.at[phase, ahead, :, left], held.at[phase, step, :, left], along_z(NZ - 1)
            ),
        )

    def spread(phase, slot):
        ids = held_ids[slot, phase * TOPK : (phase + 1) * TOPK]
        chosen = selection(ids, z * PLANE)
        for c in range(0, QUARTER, 512):
            stage[phase, slot, :, c : c + 512] = jnp.dot(
                chosen, held[phase, slot, :, c : c + 512], preferred_element_type=F32
            ).astype(BF16)
        source_pair = lax.rem(z + slot, NZ) * (PLANE // 2) + xy // 2
        at_dest = outs[phase].at[pl.ds(source_pair * SLOTS, SLOTS), my_columns]
        pltpu.make_async_copy(
            stage.at[phase, slot, pl.ds(xy * SLOTS, SLOTS)], at_dest, out_recv.at[phase]
        ).start()

        def send(step, carry):
            peer = in_plane(step)
            pltpu.make_async_remote_copy(
                src_ref=stage.at[phase, slot, pl.ds(peer * SLOTS, SLOTS)],
                dst_ref=at_dest,
                send_sem=out_send.at[phase],
                recv_sem=out_recv.at[phase],
                device_id={"dep": z * PLANE + peer},
                device_id_type=MESH,
            ).start()
            return carry

        lax.fori_loop(1, PLANE, send, 0)

    def text_spread(*slots):
        for slot in slots:
            spread(TEXT, slot)

    def attend(lanes):
        for head in range(HEADS):
            scores = jnp.dot(ks[head], qs[head, :, lanes], preferred_element_type=F32)
            below = scores - jnp.max(scores, 0, keepdims=True)
            raised = jnp.exp2(below * (math.log2(math.e) / math.sqrt(HEAD))).astype(BF16)
            product = jnp.dot(vs[head], raised, preferred_element_type=F32)
            ctx[head * HEAD : (head + 1) * HEAD, :] = product[:HEAD] / product[HEAD : HEAD + 1]
        return ctx[...].astype(BF16)

    def out_product(context, lo):
        return lax.dot_general(
            pout_ref[:, lo : lo + 384],
            context,
            (((0,), (0,)), ((), ())),
            preferred_element_type=F32,
        )

    pix_copy.wait_recv()
    for c in range(0, PATCHES, 128):
        normed[:, c : c + 128] = layer_norm(
            pix[:, c : c + 128].astype(F32), cols[0], cols[1]
        ).astype(BF16)
    loads[3].wait()
    pad = jnp.zeros((128 - HEAD, PATCHES), F32)
    queries = jnp.dot(proj_ref[0], normed[...], preferred_element_type=F32)
    for head in range(HEADS):
        part = jnp.concatenate([queries[head * HEAD : (head + 1) * HEAD], pad], 0)
        qs[head] = part.astype(BF16)
    keys = jnp.dot(proj_ref[1], normed[...], preferred_element_type=F32)
    for head in range(HEADS):
        part = jnp.concatenate([keys[head * HEAD : (head + 1) * HEAD], pad], 0)
        ks[head] = part.T.astype(BF16)
    values = jnp.dot(proj_ref[2], normed[...], preferred_element_type=F32)
    ones = jnp.ones((8, PATCHES), F32)
    for head in range(HEADS):
        part = jnp.concatenate([values[head * HEAD : (head + 1) * HEAD], ones], 0)
        vs[head] = part.astype(BF16)

    ids_copy.wait_recv()
    has = flag((TOPK, ROWS))
    held_ids[0, 0:TOPK] = jnp.where(has, ids_peer[...], ids_ref[...])
    held_ids[0, TOPK : 2 * TOPK] = jnp.where(has, ids_ref[...], ids_peer[...])
    held_ids[0, 2 * TOPK :] = jnp.full((8, ROWS), image_ref[0], jnp.int32)
    id_copies = [
        remote(held_ids.at[0], held_ids.at[NZ - step], along_z(step)) for step in range(1, NZ)
    ]

    my_rows = pl.ds(pl.multiple_of(h * 256, 256), 256)
    their_rows = pl.ds(pl.multiple_of((1 - h) * 256, 256), 256)
    arrived(hop_b)
    hop_b = z_hop_b(2)
    x_send_b(1, -1)
    arrived(across_x)
    hop_a = z_hop_a(1)
    context = attend(their_rows)
    loads[5].wait()
    part_copies = []
    for lo in range(0, V, 384):
        part_send[lo : lo + 384, :] = out_product(context, lo)
        block = pl.ds(lo, 384)
        part_copies.append(remote(part_send.at[block], part_recv.at[block], {"tp": 1 - h}))
    text_copy.wait_recv()
    held[TEXT, 0] = jnp.where(
        flag((ROWS, QUARTER)), text_peer[...].astype(F32), text_normed[:, my_columns].astype(F32)
    ).astype(BF16)
    ring = ring_hop(TEXT, 1)
    text_spread(0)
    context = attend(my_rows)
    arrived(hop_b)
    hop_b = z_hop_b(3)
    x_send_b(2, -2)
    arrived(part_copies)
    for lo in range(0, V, 384):
        block = pl.ds(lo, 384)
        part_recv[block, :] += out_product(context, lo) + pix[block, my_rows].astype(F32)
    for c in range(0, 256, 128):
        merged[:, c : c + 128] = layer_norm(part_recv[:, c : c + 128], cols[2], cols[3]).astype(
            BF16
        )
    keep = pl.ds(pl.multiple_of(p * 128, 128), 128)
    give = pl.ds(pl.multiple_of((1 - p) * 128, 128), 128)
    merged_copy = remote(merged.at[:, give], merged_peer, {"dep": other_chip})

    arrived(hop_b)
    hop_b = z_hop_b(4)
    x_send_b(3, -3)
    arrived(hop_a)
    hop_a = z_hop_a(2)
    arrived(hop_b)
    x_send_b(4)
    arrived(ring)
    arrived(id_copies)
    text_spread(1, 7)
    merged_copy.wait_recv()
    merged_mine[...] = jnp.where(
        flag((V, 128)), merged[:, keep].astype(F32), merged_peer[...].astype(F32)
    ).astype(BF16)
    lanes = pl.ds(pl.multiple_of(pair * 128, 128), 128)
    own_half = merged_mine.at[mine]
    theirs = merged_mine.at[pl.ds(pl.multiple_of((1 - h) * HALF_V, HALF_V), HALF_V)]
    place = acts.at[h, pl.ds(pl.multiple_of(p * HALF_V, HALF_V), HALF_V), lanes]
    pltpu.make_async_copy(own_half, place, acts_recv).start()
    for step in (1, 3, 2, 0):
        if step > 0:
            remote(own_half, place, {"dep": along_y(step)}, acts_recv)
        remote(theirs, place, {"dep": along_y(step), "tp": 1 - h}, acts_recv)
    arrived(hop_a)
    hop_a = z_hop_a(3)
    ring = ring_hop(TEXT, 2)
    arrived(hop_a)
    hop_a = z_hop_a(4)
    arrived(ring)
    ring = ring_hop(TEXT, 3)
    text_spread(2)
    loads[4].wait()
    scaled = text_ref[...].astype(F32) * tgain_ref[...].reshape(1, 2 * QUARTER)
    text_chosen[h] = chosen_logits(scaled, router_ref[...].reshape(2 * QUARTER, 128), ids_ref[...])
    text_gates = remote(text_chosen.at[h], text_chosen.at[h], {"tp": 1 - h})
    for slot in range(NZ):
        plane_counts[pl.ds(lax.rem(z + slot, NZ), 1), :] = held_ids[slot, 2 * TOPK : 2 * TOPK + 1]
    all_counts[xy] = plane_counts[...]

    def send_counts(step, carry):
        pltpu.make_async_remote_copy(
            src_ref=plane_counts,
            dst_ref=all_counts.at[xy],
            send_sem=counts_send,
            recv_sem=counts_recv,
            device_id={"dep": z * PLANE + in_plane(step)},
            device_id_type=MESH,
        ).start()
        return carry

    lax.fori_loop(1, PLANE, send_counts, 0)
    arrived(hop_a)
    arrived(shared)
    pltpu.make_async_copy(acts, acts, acts_recv).wait()
    text_spread(6)

    def columns_of(zs):
        total = None
        for j in range(2):
            block = weights[j, pl.ds(zs, 2)].reshape(2 * NX * OWN_COLUMNS, V)
            product = jnp.dot(block, acts[j], preferred_element_type=F32)
            total = product if total is None else total + product
        return total

    vis_copies = []
    for c in range(2):
        vis_send[c] = columns_of((1 - h) * 4 + 2 * c)
        vis_copies.append(remote(vis_send.at[c], vis_recv.at[c], {"tp": 1 - h}))
    squares = jnp.zeros((1, 2 * ROWS), F32)
    for c in range(2):
        product = columns_of(h * 4 + 2 * c)
        vis_copies[c].wait_recv()
        rounded = (product + vis_recv[c]).astype(BF16)
        vis[pl.ds(8 * c, 8)] = rounded.reshape(8, OWN_COLUMNS, 256)
        rounded = rounded.astype(F32)
        squares = squares + jnp.sum(rounded * rounded, 0, keepdims=True)
    core = 2 * y + h
    square_parts[core] = jnp.broadcast_to(squares, (8, 2 * ROWS))
    image_squares = [
        remote(
            square_parts.at[core],
            square_parts.at[core],
            {"dep": along_y(dy), "tp": h if dh == 0 else 1 - h},
        )
        for dy in range(NY)
        for dh in range(2)
        if dy + dh > 0
    ]

    def vis_block(to_y):
        return vis.at[
            pl.ds(lax.rem(to_y, 2) * 8, 8), :, pl.ds(pl.multiple_of((to_y // 2) * 128, 128), 128)
        ]

    pltpu.make_async_copy(vis_block(y), vis_all.at[:, y], vis_all_recv).start()
    for step in range(1, NY):
        to_y = lax.rem(y + step, NY)
        remote(vis_block(to_y), vis_all.at[:, y], {"dep": along_y(step)}, vis_all_recv)
    arrived(ring)
    ring = ring_hop(TEXT, 4)
    text_spread(3, 5)
    pltpu.make_async_copy(vis_all, vis_all, vis_all_recv).wait()

    hidden = vis_all[...].reshape(QUARTER, ROWS).astype(F32)
    me = p * 2 + h
    image_rows[...] = hidden.T * tgain_ref[my_columns].reshape(1, QUARTER)
    arrived(image_squares)
    squares = sum(square_parts[core, 0:1, lanes] for core in range(2 * NY))
    image_inverse = lax.rsqrt(squares / D + EPS)
    inverse = jnp.broadcast_to(image_inverse, (ROWS, ROWS)).T[:, 0:1]
    held[IMAGE, 0] = (image_rows[...] * inverse).astype(BF16)
    last_text = ring
    ring = ring_hop(IMAGE, 1)
    spread(IMAGE, 0)
    arrived(last_text)
    text_spread(4)
    gate_parts[me] = chosen_logits(image_rows[...], router_ref[p], held_ids[0, TOPK : 2 * TOPK])
    image_gates = to_unit(gate_parts)
    for step in range(1, 5):
        arrived(ring)
        if step < 4:
            ring = ring_hop(IMAGE, step + 1)
        for slot in (step, NZ - step) if step < 4 else (4,):
            spread(IMAGE, slot)
    text_gates.wait_recv()
    arrived(image_gates)
    gate_ref[...] = jnp.where(
        flag((TOPK, ROWS)),
        gate(total_of(gate_parts) * image_inverse),
        gate((text_chosen[0] + text_chosen[1]) * text_inverse),
    )

    for copy in started:
        copy.wait_send()
    others = all_counts.at[pl.ds(0, PLANE - 1)]
    pltpu.make_async_copy(others, others, counts_send).wait()
    pltpu.make_async_copy(others, others, counts_recv).wait()
    lane = lax.broadcasted_iota(jnp.int32, (NZ, ROWS), 1)
    total_counts = jnp.zeros((NZ, ROWS), jnp.int32)
    for source in range(PLANE):
        total_counts += jnp.where(lane == source, all_counts[source], 0)
    counts_ref[...] = total_counts
    for phase in (TEXT, IMAGE):
        sent = stage.at[phase, :, pl.ds(0, (PLANE - 1) * SLOTS)]
        pltpu.make_async_copy(sent, sent, out_send.at[phase]).wait()
        pltpu.make_async_copy(outs[phase], outs[phase], out_recv.at[phase]).wait()


def fused(image_count, patches, text, ids, norms, proj, pout, merger, tgain, router):
    vmem = pl.BlockSpec(memory_space=pltpu.VMEM)
    hbm = pl.BlockSpec(memory_space=pl.ANY)
    loaded = (patches, text, proj, pout, merger, router)
    rows = NZ * PLANE // 2 * SLOTS
    buffer = pltpu.VMEM((rows, 2 * QUARTER), BF16)
    copies = 128
    return pl.pallas_call(
        fused_kernel,
        out_shape=(
            buffer,
            buffer,
            pltpu.VMEM((TOPK, ROWS), F32),
            pltpu.VMEM((NZ, ROWS), jnp.int32),
        ),
        in_specs=[pl.BlockSpec(memory_space=pltpu.SMEM), hbm, hbm]
        + [vmem] * 5
        + [hbm] * 3
        + [vmem, hbm],
        out_specs=(
            vmem,
            vmem,
            vmem,
            vmem,
        ),
        scratch_shapes=[pltpu.VMEM(a.shape, a.dtype) for a in loaded]
        + [
            pltpu.VMEM((4, V, 128), F32),
            pltpu.VMEM((V, PATCHES), BF16),
            pltpu.VMEM((V, PATCHES), BF16),
            pltpu.VMEM((HEADS, 128, PATCHES), BF16),
            pltpu.VMEM((HEADS, PATCHES, 128), BF16),
            pltpu.VMEM((HEADS, HEAD + 8, PATCHES), BF16),
            pltpu.VMEM((BAND, 256), F32),
            pltpu.VMEM((V, 256), F32),
            pltpu.VMEM((V, 256), F32),
            pltpu.VMEM((V, 256), BF16),
            pltpu.VMEM((V, 128), BF16),
            pltpu.VMEM((V, 128), BF16),
            pltpu.VMEM((2, V, 256), BF16),
            pltpu.VMEM((2, NZ, NX, OWN_COLUMNS, V), BF16),
            pltpu.VMEM((2, 256, 256), F32),
            pltpu.VMEM((2, 256, 256), F32),
            pltpu.VMEM((16, OWN_COLUMNS, 256), BF16),
            pltpu.VMEM((8, NY, OWN_COLUMNS, ROWS), BF16),
            pltpu.VMEM((ROWS, QUARTER), F32),
            pltpu.VMEM((ROWS, QUARTER), BF16),
            pltpu.VMEM((ROWS, 2 * QUARTER), BF16),
            pltpu.VMEM((2, 8, ROWS), F32),
            pltpu.VMEM((2, TOPK, ROWS), F32),
            pltpu.VMEM((TOPK, ROWS), jnp.int32),
            pltpu.VMEM((NZ, 2 * TOPK + 8, ROWS), jnp.int32),
            pltpu.VMEM((NZ, ROWS), jnp.int32),
            pltpu.VMEM((PLANE, NZ, ROWS), jnp.int32),
            pltpu.VMEM((2, NZ, ROWS, QUARTER), BF16),
            pltpu.VMEM((2, NZ, PLANE * SLOTS, QUARTER), BF16),
            pltpu.VMEM((2 * NY, 8, 2 * ROWS), F32),
            pltpu.VMEM((4, TOPK, ROWS), F32),
            pltpu.SemaphoreType.DMA((6,)),
            pltpu.SemaphoreType.DMA((copies,)),
            pltpu.SemaphoreType.DMA((copies,)),
            pltpu.SemaphoreType.DMA,
            pltpu.SemaphoreType.DMA,
            pltpu.SemaphoreType.DMA((2,)),
            pltpu.SemaphoreType.DMA((2,)),
            pltpu.SemaphoreType.DMA,
            pltpu.SemaphoreType.DMA,
        ],
        compiler_params=pltpu.CompilerParams(
            collective_id=0, has_side_effects=True, vmem_limit_bytes=46 * 1024 * 1024
        ),
    )(image_count, patches, text, ids, *norms, proj, pout, merger, tgain, router)


def interleave_kernel(counts_ref, text_ref, image_ref, gate_ref, out_ref, gate_out, sem):
    def pair_rows(ref, k):
        return ref.at[pl.ds(pl.multiple_of(k * SLOTS, SLOTS), SLOTS)]

    def step(k, carry):
        first = counts_ref[k // (PLANE // 2), 2 * lax.rem(k, PLANE // 2)]
        pltpu.make_async_copy(pair_rows(text_ref, k), pair_rows(out_ref, 2 * k + first), sem).start(
            priority=0
        )
        pltpu.make_async_copy(
            pair_rows(image_ref, k), pair_rows(out_ref, 2 * k + 1 - first), sem
        ).start(priority=1)
        return carry

    lax.fori_loop(0, NZ * PLANE // 2, step, 0)
    gate_out[...] = gate_ref[...]
    pltpu.make_async_copy(out_ref, out_ref, sem).wait()


def interleave(counts, text_rows, image_rows, gates):
    vmem = pl.BlockSpec(memory_space=pltpu.VMEM)
    held = pl.BlockSpec(memory_space=pl.ANY)
    return pl.pallas_call(
        interleave_kernel,
        out_shape=(
            jax.ShapeDtypeStruct((2 * text_rows.shape[0], text_rows.shape[1]), BF16),
            jax.ShapeDtypeStruct(gates.shape, F32),
        ),
        in_specs=[pl.BlockSpec(memory_space=pltpu.SMEM), held, held, vmem],
        out_specs=(held, vmem),
        scratch_shapes=[pltpu.SemaphoreType.DMA],
        compiler_params=pltpu.CompilerParams(vmem_limit_bytes=4 * 1024 * 1024),
    )(counts, text_rows, image_rows, gates)


def per_device(
    patches,
    image_count,
    text_tokens,
    norm_gain,
    norm_bias,
    patch_proj,
    patch_out,
    merge_gain,
    merge_bias,
    merger,
    token_gain,
    router,
    expert_ids,
):
    text_rows, image_rows, gates, counts = fused(
        image_count,
        patches.T,
        text_tokens,
        expert_ids.T,
        (norm_gain, norm_bias, merge_gain, merge_bias),
        patch_proj.transpose(1, 2, 0),
        patch_out,
        merger.transpose(0, 2, 1),
        token_gain,
        router.reshape(2, QUARTER, router.shape[1]),
    )
    dispatched, gate_probs = interleave(counts, text_rows, image_rows, gates)
    return dispatched[None], gate_probs.T


def solution(mesh):
    return jax.shard_map(
        per_device,
        mesh=mesh,
        in_specs=(
            P("dep", "tp"),
            P("dep"),
            P("dep", "tp"),
            P(),
            P(),
            P(None, None, "tp"),
            P("tp", None),
            P(),
            P(),
            P(None, "tp", "dep"),
            P("tp"),
            P("tp", None),
            P("dep", None),
        ),
        out_specs=(P("dep", None, "tp"), P("dep", None)),
        check_vma=False,
    )
```
